32 devices in a mesh: section: 4 (over z), tp: 8 (over y, x, core).
Axes of the slice: x: 2, y: 2, z: 4, core: 2. Of those that a mesh axis runs over, the one named last changes fastest.
Arguments:
- teacher_rows: bfloat16 [4, 256, 8192], P('section', 'tp'), may hold values from -72 to 72
- norm_gain: float32 [4, 8192], P('section'), may hold values from 0.1 to 1.9
- query_weight: bfloat16 [4, 8192, 8192], P('section', None, 'tp'), may hold values from -2.762136 to 2.762136
- keys_values: bfloat16 [4, 2, 8192, 1024], P('section', None, None, 'tp'), may hold values from -0.071815532 to 0.071815532
- output_weight: bfloat16 [4, 8192, 8192], P('section', 'tp'), may hold values from -0.5 to 0.5
- doc_start: int32 [4], P('section'), may hold values from 1 to 255
- student_rows: bfloat16 [4, 256, 4096], P('section', 'tp'), may hold values from -30 to 30
- projector: bfloat16 [4096, 8192], P('tp', 'section'), may hold values from -1 to 2
Outputs:
- teacher_next: bfloat16 [4, 256, 8192], P('section', 'tp')
- distill_loss: float32 [], replicated
- grad_student: float32 [4, 256, 4096], P('section', 'tp')
- grad_projector: float32 [4096, 8192], P('tp', 'section')
The draws below stay inside these ranges and needn't reach their ends.
All inputs are finite; a program needn't handle non-finite values.
Results may differ from the reference program's by a relative error of at most 0.02.
Values may be sent and summed in bfloat16 or wider, within the bound.
A program may use at most 128 MiB of HBM per device.

```python
import math
import jax
import jax.numpy as jnp
from jax import lax

DT = 8192
DS = 4096
QH = 64
KVH = 8
HD = 128
TROWS = 256
N_SECTION = 4
N_TP = 8


def common_keys(key):
    raw = jax.random.normal(jax.random.fold_in(key, 101), (N_SECTION, 2, DT, KVH * HD), jnp.float32)
    return jnp.clip(raw, -6.0, 6.0) * (1.0 / math.sqrt(DT))


def draw_keys_values(key, part):
    return common_keys(key).astype(jnp.bfloat16)


def draw_query_weight(key, part):
    base = jax.random.normal(jax.random.fold_in(key, 102), (N_SECTION, DT, QH * HD), jnp.float32)
    base = jnp.clip(base, -6.0, 6.0) * (1.0 / math.sqrt(DT))
    return base.astype(jnp.bfloat16)


def student_parts(key):
    shape = (N_SECTION, TROWS, DS)
    row_scale = jnp.exp(jax.random.uniform(jax.random.fold_in(key, 11), (N_SECTION, TROWS, 1), jnp.float32, minval=-1.15, maxval=1.15))
    col_scale = jnp.exp(jax.random.uniform(jax.random.fold_in(key, 12), (1, 1, DS), jnp.float32, minval=-0.35, maxval=0.35))
    noise = jnp.clip(jax.random.normal(jax.random.fold_in(key, 13), shape, jnp.float32), -6.0, 6.0)
    return (noise * col_scale, row_scale)


def draw_student_rows(key, part):
    unit_rows, row_scale = student_parts(key)
    return (unit_rows * row_scale).astype(jnp.bfloat16)


def draw_teacher_rows(key, part):
    shape = (N_SECTION, TROWS, DT)
    unit_rows, student_scale = student_parts(key)
    column_source = jnp.arange(DT, dtype=jnp.int32) % DS
    aligned = jnp.take(unit_rows, column_source, axis=2)
    row_fraction = (jnp.arange(TROWS, dtype=jnp.int32).astype(jnp.float32) / TROWS).reshape(1, TROWS, 1)
    section_fraction = (jnp.arange(N_SECTION, dtype=jnp.int32).astype(jnp.float32) / N_SECTION).reshape(N_SECTION, 1, 1)
    jitter = jax.random.uniform(jax.random.fold_in(key, 5), (N_SECTION, TROWS, 1), jnp.float32, minval=-0.2, maxval=0.2)
    amount = 1.6 - 1.2 * row_fraction - 1.2 * section_fraction + jitter
    row_scale = jnp.exp(jax.random.uniform(jax.random.fold_in(key, 1), (N_SECTION, TROWS, 1), jnp.float32, minval=-1.15, maxval=1.15))
    col_scale = jnp.exp(jax.random.uniform(jax.random.fold_in(key, 2), (1, 1, DT), jnp.float32, minval=-0.35, maxval=0.35))
    noise = jnp.clip(jax.random.normal(jax.random.fold_in(key, 3), shape, jnp.float32), -6.0, 6.0)
    return ((amount * aligned + 0.5 * noise) * row_scale * col_scale).astype(jnp.bfloat16)


def draw_projector(key, part):
    rows_index = jnp.arange(DS, dtype=jnp.int32)
    cols_index = jnp.arange(DT, dtype=jnp.int32) % DS
    tiled = (rows_index[:, None] == cols_index[None, :]).astype(jnp.float32)
    noise = jnp.clip(jax.random.normal(jax.random.fold_in(key, 21), (DS, DT), jnp.float32), -6.0, 6.0)
    return (tiled + noise * (0.5 / math.sqrt(DS))).astype(jnp.bfloat16)


def touch_ends(values, own_key, least, largest):
    extent = values.shape
    index_at = [jax.random.randint(jax.random.fold_in(own_key, axis), (), 0, extent[axis]) for axis in range(len(extent))]
    values = values.at[tuple(index_at)].set(least)
    longest = extent.index(max(extent))
    index_at[longest] = (index_at[longest] + 1) % extent[longest]
    return values.at[tuple(index_at)].set(largest)


def shard_levels(stream_key, shape, cuts, low, top_value):
    gain = 1.0
    for position, parts in cuts:
        heights = jax.random.uniform(jax.random.fold_in(jax.random.fold_in(stream_key, 6), position), (parts,), jnp.float32, low / len(cuts), top_value / len(cuts))
        gain = gain * jnp.repeat(jnp.exp(heights), shape[position] // parts).reshape((-1,) + (1,) * (len(shape) - 1 - position))
    return gain


def scatter_about(own_key, shape, scale, most, split=(), held_as=jnp.bfloat16):
    values = jax.random.normal(own_key, shape, jnp.float32) * scale
    if len(split) > 0:
        values = shard_levels(own_key, shape, split, -0.22, 0.18) * values
    return jnp.clip(values, min=-most, max=most).astype(held_as)


def setup_inputs(seed: int = 0) -> dict:
    key_list = jax.random.split(jax.random.key(seed), 9)
    teacher_rows = draw_teacher_rows(jax.random.fold_in(key_list[8], 71), 0)
    norm_gain = jnp.clip(1.0 + 0.18 * jax.random.normal(key_list[1], (N_SECTION, DT), jnp.float32), 0.1, 1.9)
    query_weight = draw_query_weight(jax.random.fold_in(key_list[8], 71), 0)
    keys_values = draw_keys_values(jax.random.fold_in(key_list[8], 71), 0)
    output_weight = scatter_about(key_list[4], (N_SECTION, QH * HD, DT), HD ** -0.5, 0.5, ((0, 4), (1, 8)))
    doc_start = touch_ends(jax.random.randint(key_list[5], (N_SECTION,), 1, TROWS), jax.random.fold_in(key_list[5], 1), 1, TROWS - 1).astype(jnp.int32)
    student_rows = draw_student_rows(jax.random.fold_in(key_list[8], 71), 0)
    projector = draw_projector(jax.random.fold_in(key_list[8], 71), 0)
    return {"teacher_rows": teacher_rows, "norm_gain": norm_gain, "query_weight": query_weight, "keys_values": keys_values, "output_weight": output_weight, "doc_start": doc_start, "student_rows": student_rows, "projector": projector}


LOSS_WEIGHT = 64.0
NORM_EPS = 1e-05
COS_EPS = 1e-06

def round_bf16(values):
    return lax.optimization_barrier(values.astype(jnp.bfloat16)).astype(jnp.float32)

def teacher_layer(span_rows, gain_row, query_mat, key_mat, value_mat, out_mat, first_new):
    rows_float = span_rows.astype(jnp.float32)
    mean_square = lax.optimization_barrier(jnp.mean(rows_float * rows_float, axis=1, keepdims=True))
    normed = (rows_float * lax.rsqrt(mean_square + NORM_EPS) * gain_row[None, :]).astype(jnp.bfloat16)
    queries = jnp.dot(normed, query_mat, preferred_element_type=jnp.float32).astype(jnp.bfloat16)
    keys_all = jnp.dot(normed, key_mat, preferred_element_type=jnp.float32).astype(jnp.bfloat16)
    values_all = jnp.dot(normed, value_mat, preferred_element_type=jnp.float32).astype(jnp.bfloat16)
    row_total = span_rows.shape[0]
    group = QH // KVH
    query_heads = queries.astype(jnp.float32).reshape(row_total, KVH, group, HD)
    key_heads = keys_all.astype(jnp.float32).reshape(row_total, KVH, HD)
    value_heads = values_all.astype(jnp.float32).reshape(row_total, KVH, HD)
    scale = 1.0 / math.sqrt(HD)
    scores = jnp.einsum('qegd,ked->egqk', query_heads, key_heads) * scale
    positions = jnp.arange(row_total, dtype=jnp.int32)
    after_start = positions >= first_new
    visible = (positions[None, :] <= positions[:, None]) & (after_start[None, :] == after_start[:, None])
    scores = jnp.where(visible, scores, -1e+30)
    row_max = lax.optimization_barrier(jnp.max(scores, axis=-1, keepdims=True))
    expo = jnp.where(visible, jnp.exp(scores - row_max), 0.0)
    weights = (expo / lax.optimization_barrier(jnp.sum(expo, axis=-1, keepdims=True))).astype(jnp.bfloat16)
    mixed = jnp.einsum('egqk,ked->qegd', weights.astype(jnp.float32), value_heads)
    mixed = mixed.astype(jnp.bfloat16).reshape(row_total, QH * HD)
    group_cols = QH * HD // N_TP
    mixed_groups = jnp.transpose(mixed.reshape(row_total, N_TP, group_cols), (1, 0, 2))
    out_groups = out_mat.reshape(N_TP, group_cols, DT)

    def group_term(operands):
        return jnp.dot(operands[0], operands[1], preferred_element_type=jnp.float32).astype(jnp.bfloat16)
    partials = lax.map(group_term, (mixed_groups, out_groups))
    attn_sum = lax.optimization_barrier(jnp.sum(lax.optimization_barrier(partials).astype(jnp.float32), axis=0))
    return (rows_float + attn_sum).astype(jnp.bfloat16)

def cosine_step(inner, own_sq, target_sq, student_proj, target):
    inv_own = lax.rsqrt(own_sq + COS_EPS)
    inv_target = lax.rsqrt(target_sq + COS_EPS)
    cosine = inner * inv_own * inv_target
    slope = LOSS_WEIGHT * ((inner * inv_target * inv_own * inv_own * inv_own)[:, None] * student_proj - target * (inv_own * inv_target)[:, None])
    return (cosine, slope.astype(jnp.bfloat16))

def reference(teacher_rows, norm_gain, query_weight, keys_values, output_weight, doc_start, student_rows, projector):
    outputs = []
    for section_index in range(N_SECTION):
        outputs.append(teacher_layer(teacher_rows[section_index], norm_gain[section_index], query_weight[section_index], keys_values[section_index, 0], keys_values[section_index, 1], output_weight[section_index], doc_start[section_index]))
    teacher_next = jnp.stack(outputs, axis=0)
    token_count = N_SECTION * TROWS
    token_rows = student_rows.reshape(token_count, DS)
    target = teacher_next.reshape(token_count, DT).astype(jnp.float32)
    student_proj = jnp.dot(token_rows, projector, preferred_element_type=jnp.float32)
    inner = lax.optimization_barrier(jnp.sum(student_proj * target, axis=1))
    own_sq = lax.optimization_barrier(jnp.sum(student_proj * student_proj, axis=1))
    target_sq = lax.optimization_barrier(jnp.sum(target * target, axis=1))
    cosine, slope = cosine_step(inner, own_sq, target_sq, student_proj, target)
    distill_loss = jnp.mean(1.0 - cosine)
    grad_student = jnp.dot(slope, projector.T, preferred_element_type=jnp.float32).reshape(N_SECTION, TROWS, DS)
    grad_projector = jnp.dot(token_rows.T, slope, preferred_element_type=jnp.float32)
    return (teacher_next, distill_loss, grad_student, grad_projector)
```

```python
import functools
import math

import jax
import jax.numpy as jnp
from jax import lax
from jax.experimental import pallas as pl
from jax.experimental.pallas import tpu as pltpu
from jax.sharding import PartitionSpec as P

KVH = 8
HD = 128


LOSS_WEIGHT = 64.0
NORM_EPS = 1e-05
COS_EPS = 1e-06


def as_sent(value):
    return jax.tree.map(lambda a: a.astype(jnp.bfloat16) if a.dtype == jnp.float32 else a, value)


def partner(value, axis, apart):
    mask = 2**apart
    pairs = [(source, source ^ mask) for source in range(lax.axis_size(axis))]
    return lax.ppermute(value, axis, pairs)


def round_bf16(values):
    return lax.optimization_barrier(values.astype(jnp.bfloat16)).astype(jnp.float32)


def join_halves(mine, other, low_side):
    return jnp.where(
        low_side, jnp.concatenate([mine, other], axis=1), jnp.concatenate([other, mine], axis=1)
    )


def cosine_step(inner, own_sq, target_sq, student_proj, target):
    inv_own = lax.rsqrt(own_sq + COS_EPS)
    inv_target = lax.rsqrt(target_sq + COS_EPS)
    cosine = inner * inv_own * inv_target
    slope = LOSS_WEIGHT * (
        (inner * inv_target * inv_own * inv_own * inv_own)[:, None] * student_proj
        - target * (inv_own * inv_target)[:, None]
    )
    return (cosine, slope.astype(jnp.bfloat16))


def attend(queries, keys_full, values_full, first_new):
    row_total = queries.shape[0]
    kv_heads = keys_full.shape[1] // HD
    group = queries.shape[1] // HD // kv_heads
    query_heads = queries.reshape(row_total, kv_heads, group, HD)
    key_heads = keys_full.reshape(row_total, kv_heads, HD)
    value_heads = values_full.reshape(row_total, kv_heads, HD)
    scale = 1.0 / math.sqrt(HD)
    scores = (
        jnp.einsum("qegd,ked->egqk", query_heads, key_heads, preferred_element_type=jnp.float32)
        * scale
    )
    positions = jnp.arange(row_total, dtype=jnp.int32)
    after_start = positions >= first_new
    visible = (positions[None, :] <= positions[:, None]) & (
        after_start[None, :] == after_start[:, None]
    )
    scores = jnp.where(visible, scores, -1e30)
    row_max = jnp.max(scores, axis=-1, keepdims=True)
    expo = jnp.where(visible, jnp.exp(scores - row_max), 0.0)
    weights = (expo / jnp.sum(expo, axis=-1, keepdims=True)).astype(jnp.bfloat16)
    mixed = jnp.einsum("egqk,ked->qegd", weights, value_heads, preferred_element_type=jnp.float32)
    return mixed.astype(jnp.bfloat16).reshape(row_total, queries.shape[1])


def shards(
    teacher_rows,
    norm_gain,
    query_weight,
    keys_values,
    output_weight,
    doc_start,
    student_rows,
    projector,
):
    span_rows = teacher_rows[0]
    tp_count = lax.axis_size("tp")
    tp_position = lax.axis_index("tp")
    rows_float = span_rows.astype(jnp.float32)
    mean_square = jnp.mean(rows_float * rows_float, axis=1, keepdims=True)
    normed = (rows_float * lax.rsqrt(mean_square + NORM_EPS) * norm_gain[0][None, :]).astype(
        jnp.bfloat16
    )
    query_local = query_weight[0]
    key_local = keys_values[0, 0]
    value_local = keys_values[0, 1]
    share_count = max(1, tp_count // KVH)
    bit_total = share_count.bit_length() - 1
    query_cols = query_local.shape[1]
    key_cols = key_local.shape[1]
    block_rows = lax.all_gather(normed, "tp", axis=0, tiled=True)
    query_part = jnp.dot(block_rows, query_local, preferred_element_type=jnp.float32).astype(
        jnp.bfloat16
    )
    key_part = jnp.dot(block_rows, key_local, preferred_element_type=jnp.float32).astype(
        jnp.bfloat16
    )
    value_part = jnp.dot(block_rows, value_local, preferred_element_type=jnp.float32).astype(
        jnp.bfloat16
    )
    projected = jnp.concatenate([query_part, key_part, value_part], axis=1)
    queries = projected[:, :query_cols]
    keys_full = projected[:, query_cols : query_cols + key_cols]
    values_full = projected[:, query_cols + key_cols :]
    for bit_index in range(bit_total):
        other_key, other_value = (
            partner(as_sent(keys_full), "tp", bit_index).astype(keys_full.dtype),
            partner(as_sent(values_full), "tp", bit_index).astype(values_full.dtype),
        )
        low_side = tp_position // 2**bit_index % 2 == 0
        keys_full = join_halves(keys_full, other_key, low_side)
        values_full = join_halves(values_full, other_value, low_side)
    mixed_heads = attend(queries, keys_full, values_full, doc_start[0])
    out_local = output_weight[0]
    block = mixed_heads
    attn_sum = lax.psum_scatter(
        round_bf16(jnp.dot(block, out_local, preferred_element_type=jnp.float32)).astype(
            jnp.bfloat16
        ),
        "tp",
        scatter_dimension=0,
        tiled=True,
    ).astype(jnp.float32)
    teacher_next = (rows_float + attn_sum).astype(jnp.bfloat16)
    contract_last = (((1,), (1,)), ((), ()))
    contract_pair = (((0, 1), (0, 1)), ((), ()))
    gathered = lax.all_gather(student_rows, "section", axis=0, tiled=True)
    token_count = gathered.shape[0] * gathered.shape[1]
    token_rows = gathered.reshape(token_count, gathered.shape[2])
    arrived = lax.all_to_all(teacher_next[None], "section", split_axis=2, concat_axis=0, tiled=True)
    target = arrived.reshape(token_count, arrived.shape[2]).astype(jnp.float32)
    student_proj = jnp.dot(
        token_rows,
        lax.all_gather(projector, "tp", axis=0, tiled=True),
        preferred_element_type=jnp.float32,
    )
    inner, own_sq, target_sq = lax.psum(
        (
            jnp.sum(student_proj * target, axis=1),
            jnp.sum(student_proj * student_proj, axis=1),
            jnp.sum(target * target, axis=1),
        ),
        "section",
    )
    cosine, slope = cosine_step(inner, own_sq, target_sq, student_proj, target)
    loss_total = lax.psum(jnp.sum(1.0 - cosine), "tp")
    distill_loss = loss_total / (token_count * tp_count)
    row_terms = lax.dot_general(
        slope,
        lax.all_gather(projector, "tp", axis=0, tiled=True),
        contract_last,
        preferred_element_type=jnp.float32,
    )
    grad_local = lax.psum_scatter(
        row_terms.astype(jnp.bfloat16), "section", scatter_dimension=0, tiled=True
    ).astype(jnp.float32)
    by_column = lax.all_to_all(gathered, "tp", split_axis=2, concat_axis=1, tiled=True)
    slope_stacked = slope.reshape(gathered.shape[0], gathered.shape[1], slope.shape[1])
    block = by_column
    grad_proj = lax.dot_general(
        block,
        lax.all_gather(slope_stacked, "tp", axis=1, tiled=True),
        contract_pair,
        preferred_element_type=jnp.float32,
    )
    return (teacher_next[None], distill_loss, grad_local[None], grad_proj)


MESH = pl.DeviceIdType.MESH
F32 = jnp.float32
BF16 = jnp.bfloat16
SECTIONS = 4
TPS = 8
VMEM_LIMIT = 58 * 1024 * 1024


def places():
    section = lax.axis_index("section")
    tp = lax.axis_index("tp")
    core = tp % 2
    x = (tp // 2) % 2
    y = tp // 4
    sib = tp + 1 - 2 * core
    xn = tp + 2 - 4 * x
    yn = tp + 4 - 8 * y
    first = (1 - core) * xn + core * yn
    second = core * xn + (1 - core) * yn
    diag = xn + 4 - 8 * y
    return section, tp, core, x, y, sib, first, second, diag


def greet_all(section, tp):
    barrier = pltpu.get_barrier_semaphore()
    me = section * TPS + tp

    def one(step, carry):
        other = (me + step) % (SECTIONS * TPS)
        pl.semaphore_signal(
            barrier, inc=1, device_id=(other // TPS, other % TPS), device_id_type=MESH
        )
        return carry

    lax.fori_loop(1, SECTIONS * TPS, one, 0)
    pl.semaphore_wait(barrier, SECTIONS * TPS - 1)


def greet(peers):
    barrier = pltpu.get_barrier_semaphore()
    for peer in peers:
        pl.semaphore_signal(barrier, inc=1, device_id=peer, device_id_type=MESH)
    pl.semaphore_wait(barrier, len(peers))


def gather_ops(buf, rows, send_sem, recv_sem):
    section, tp, core, x, y, sib, first, second, diag = places()

    def copy(kind, chunk, owner, target):
        place = buf.at[chunk, pl.ds(pl.multiple_of(owner * rows, rows), rows)]
        return pltpu.make_async_remote_copy(
            src_ref=place,
            dst_ref=place,
            send_sem=send_sem.at[kind, chunk],
            recv_sem=recv_sem.at[kind, chunk],
            device_id=(section, target),
            device_id_type=MESH,
        )

    def begin(chunk):
        copy(0, chunk, tp, first).start()
        copy(1, chunk, tp, second).start()
        copy(2, chunk, tp, sib).start()

    def forward(chunk):
        copy(0, chunk, tp, first).wait_recv()
        copy(3, chunk, first, second).start()
        copy(4, chunk, first, sib).start()
        copy(1, chunk, tp, second).wait_recv()
        copy(5, chunk, second, sib).start()

    def across(chunk):
        copy(3, chunk, first, second).wait_recv()
        copy(6, chunk, diag, sib).start()

    def arrive(chunk):
        copy(2, chunk, tp, sib).wait_recv()
        copy(4, chunk, first, sib).wait_recv()
        copy(5, chunk, second, sib).wait_recv()
        copy(6, chunk, diag, sib).wait_recv()

    def drain(chunk):
        for kind in range(7):
            copy(kind, chunk, tp, sib).wait_send()

    return begin, forward, across, arrive, drain


def project_kernel(
    normed, student, wq_hbm, wkv_hbm,
    qkv, feats,
    buf, wq, wkv, acc, acc_k, acc_v,
    g_send, g_recv, s_send, s_recv, w_sem,
):
    section, tp, core, x, y, sib, first, second, diag = places()
    chunks, width = buf.shape[0], buf.shape[2]
    rows = normed.shape[0]
    part = feats.shape[3]
    me = section * TPS + tp

    def wq_copy(c):
        at = pl.ds(pl.multiple_of(c * width, width), width)
        return pltpu.make_async_copy(wq_hbm.at[at], wq.at[at], w_sem.at[0, c])

    def wkv_copy(c):
        at = pl.ds(pl.multiple_of(c * width, width), width)
        return pltpu.make_async_copy(wkv_hbm.at[:, at], wkv.at[:, at], w_sem.at[1, c])

    def load(c, carry):
        wq_copy(c).start()
        wkv_copy(c).start()
        at = pl.ds(pl.multiple_of(c * width, width), width)
        buf[c, pl.ds(pl.multiple_of(tp * rows, rows), rows)] = normed[:, at]
        return carry

    lax.fori_loop(0, chunks, load, 0)
    feats[tp, section] = student[:, pl.ds(pl.multiple_of(tp * part, part), part)]
    acc[...] = jnp.zeros_like(acc)
    acc_k[...] = jnp.zeros_like(acc_k)
    acc_v[...] = jnp.zeros_like(acc_v)
    greet_all(section, tp)
    begin, forward, across, arrive, drain = gather_ops(buf, rows, g_send, g_recv)

    def s_copy(step):
        other = (me + step) % (SECTIONS * TPS)
        to_section, to_tp = other // TPS, other % TPS
        return pltpu.make_async_remote_copy(
            src_ref=student.at[:, pl.ds(pl.multiple_of(to_tp * part, part), part)],
            dst_ref=feats.at[tp, section],
            send_sem=s_send.at[step],
            recv_sem=s_recv.at[step],
            device_id=(to_section, to_tp),
            device_id_type=MESH,
        )

    def start_gather(c, carry):
        begin(c)
        return carry

    lax.fori_loop(0, chunks, start_gather, 0)

    def start_student(step, carry):
        s_copy(step).start()
        return carry

    lax.fori_loop(1, SECTIONS * TPS, start_student, 0)

    def step(i, carry):
        @pl.when(i < chunks)
        def _():
            forward(i)

        @pl.when((i >= 1) & (i < chunks + 1))
        def _():
            across(i - 1)

        @pl.when(i >= 2)
        def _():
            c = i - 2
            arrive(c)
            wq_copy(c).wait()
            wkv_copy(c).wait()
            at = pl.ds(pl.multiple_of(c * width, width), width)
            block = buf[c]
            acc[...] += jnp.dot(block, wq[at], preferred_element_type=F32)
            acc_k[...] += jnp.dot(block, wkv[0, at], preferred_element_type=F32)
            acc_v[...] += jnp.dot(block, wkv[1, at], preferred_element_type=F32)

        return carry

    lax.fori_loop(0, chunks + 2, step, 0)
    q_cols = acc.shape[1]
    k_cols = acc_k.shape[1]
    qkv[:, :q_cols] = acc[...].astype(BF16)
    qkv[:, q_cols : q_cols + k_cols] = acc_k[...].astype(BF16)
    qkv[:, q_cols + k_cols :] = acc_v[...].astype(BF16)

    def finish(c, carry):
        drain(c)
        return carry

    lax.fori_loop(0, chunks, finish, 0)

    def finish_student(step, carry):
        s_copy(step).wait()
        return carry

    lax.fori_loop(1, SECTIONS * TPS, finish_student, 0)


def project(normed, student, wq, wkv):
    rows, depth = normed.shape
    total = rows * TPS
    q_cols, k_cols = wq.shape[1], wkv.shape[2]
    chunks = 8
    part = student.shape[1] // TPS
    vmem = pl.BlockSpec(memory_space=pltpu.VMEM)
    hbm = pl.BlockSpec(memory_space=pl.ANY)
    return pl.pallas_call(
        project_kernel,
        out_shape=(
            jax.ShapeDtypeStruct((total, q_cols + 2 * k_cols), BF16),
            jax.ShapeDtypeStruct((TPS, SECTIONS, rows, part), BF16),
        ),
        in_specs=[vmem, vmem, hbm, hbm],
        out_specs=(vmem, vmem),
        scratch_shapes=[
            pltpu.VMEM((chunks, total, depth // chunks), BF16),
            pltpu.VMEM(wq.shape, BF16),
            pltpu.VMEM(wkv.shape, BF16),
            pltpu.VMEM((total, q_cols), F32),
            pltpu.VMEM((total, k_cols), F32),
            pltpu.VMEM((total, k_cols), F32),
            pltpu.SemaphoreType.DMA((7, chunks)),
            pltpu.SemaphoreType.DMA((7, chunks)),
            pltpu.SemaphoreType.DMA((SECTIONS * TPS,)),
            pltpu.SemaphoreType.DMA((SECTIONS * TPS,)),
            pltpu.SemaphoreType.DMA((2, chunks)),
        ],
        compiler_params=pltpu.CompilerParams(
            collective_id=0, has_side_effects=True, vmem_limit_bytes=VMEM_LIMIT
        ),
        name="gather_project",
    )(normed, student, wq, wkv)


def scatter_kernel(
    teacher, lhs, rhs_hbm, *refs,
):
    if teacher:
        resid, out, shared = refs[:3]
        refs = refs[3:]
    else:
        out = refs[0]
        refs = refs[1:]
    rhs, part, sib_buf, pair, got1, half, got2, sends, recvs, w_sem = refs[:10]
    if teacher:
        z_send, z_recv = refs[10:]
    section, tp, core, x, y, sib, first, second, diag = places()
    chunks, _, m, width = part.shape
    f_mine = (1 - core) * x + core * y
    g_mine = core * x + (1 - core) * y

    def column(i):
        if teacher:
            return (i % SECTIONS) * (chunks // SECTIONS) + i // SECTIONS
        return i

    def columns(i):
        return pl.ds(pl.multiple_of(column(i) * width, width), width)

    def w_copy(i):
        return pltpu.make_async_copy(rhs_hbm.at[:, columns(i)], rhs.at[i], w_sem.at[i])

    def load(i, carry):
        w_copy(i).start()
        return carry

    lax.fori_loop(0, chunks, load, 0)
    peers = [(section, sib), (section, first), (section, second)]
    if teacher:
        peers += [((section + d) % SECTIONS, tp) for d in range(1, SECTIONS)]
    greet(peers)

    def remote(kind, i, source, landing, target):
        return pltpu.make_async_remote_copy(
            src_ref=source,
            dst_ref=landing,
            send_sem=sends.at[kind, i],
            recv_sem=recvs.at[kind, i],
            device_id=(section, target),
            device_id_type=MESH,
        )

    def to_sib(i):
        return remote(0, i, part.at[i, pl.ds(4 * (1 - core), 4)], sib_buf.at[i], sib)

    def to_first(i):
        return remote(1, i, pair.at[i, 1 - f_mine], got1.at[i], first)

    def to_second(i):
        return remote(2, i, half.at[i, 1 - g_mine], got2.at[i], second)

    def to_z(i, d):
        return pltpu.make_async_remote_copy(
            src_ref=out.at[:, columns(i)],
            dst_ref=shared.at[section, :, pl.ds(pl.multiple_of((i // SECTIONS) * width, width), width)],
            send_sem=z_send.at[i],
            recv_sem=z_recv.at[section, i // SECTIONS],
            device_id=(i % SECTIONS, tp),
            device_id_type=MESH,
        )

    def from_z(other, h):
        place = shared.at[other, :, pl.ds(pl.multiple_of(h * width, width), width)]
        return pltpu.make_async_remote_copy(
            src_ref=place,
            dst_ref=place,
            send_sem=z_send.at[0],
            recv_sem=z_recv.at[other, h],
            device_id=(other, tp),
            device_id_type=MESH,
        )

    def stage_a(i):
        w_copy(i).wait()
        block = jnp.dot(lhs[...], rhs[i], preferred_element_type=F32).astype(BF16)
        for t in range(TPS):
            yy, xx, cc = t // 4, (t // 2) % 2, t % 2
            slot = 4 * cc + 2 * (yy if cc else xx) + (xx if cc else yy)
            part[i, slot] = block[t * m : (t + 1) * m]
        to_sib(i).start()

    def stage_b(i):
        to_sib(i).wait_recv()
        for f in range(2):
            for g in range(2):
                mine = part[i, 4 * core + 2 * f + g].astype(F32)
                pair[i, f, g] = (mine + sib_buf[i, 2 * f + g].astype(F32)).astype(BF16)
        to_first(i).start()

    def stage_c(i):
        to_first(i).wait_recv()
        for g in range(2):
            half[i, g] = (pair[i, f_mine, g].astype(F32) + got1[i, g].astype(F32)).astype(BF16)
        to_second(i).start()

    def stage_d(i):
        to_second(i).wait_recv()
        total = half[i, g_mine].astype(F32) + got2[i].astype(F32)
        if not teacher:
            out[:, columns(i)] = total
            return
        value = (resid[:, columns(i)].astype(F32) + total).astype(BF16)
        out[:, columns(i)] = value

        @pl.when(i % SECTIONS == section)
        def _():
            at = pl.ds(pl.multiple_of((i // SECTIONS) * width, width), width)
            shared[section, :, at] = value

        @pl.when(i % SECTIONS != section)
        def _():
            to_z(i, 0).start()

    ends = (0, 1, 3, 5)

    def step(i, carry):
        for late, stage in zip(ends, (stage_a, stage_b, stage_c, stage_d)):

            @pl.when((i >= late) & (i < chunks + late))
            def _():
                stage(i - late)

        return carry

    lax.fori_loop(0, chunks + ends[-1], step, 0)

    def finish(i, carry):
        to_sib(i).wait_send()
        to_first(i).wait_send()
        to_second(i).wait_send()
        if teacher:

            @pl.when(i % SECTIONS != section)
            def _():
                to_z(i, 0).wait_send()

            @pl.when(i % SECTIONS != section)
            def _():
                from_z(i % SECTIONS, i // SECTIONS).wait_recv()

        return carry

    lax.fori_loop(0, chunks, finish, 0)


def scatter(lhs, rhs, resid=None):
    teacher = resid is not None
    depth, cols = rhs.shape
    m = lhs.shape[0] // TPS
    chunks = 8
    width = cols // chunks
    vmem = pl.BlockSpec(memory_space=pltpu.VMEM)
    hbm = pl.BlockSpec(memory_space=pl.ANY)
    scratch = [
        pltpu.VMEM((chunks, depth, width), BF16),
        pltpu.VMEM((chunks, TPS, m, width), BF16),
        pltpu.VMEM((chunks, 4, m, width), BF16),
        pltpu.VMEM((chunks, 2, 2, m, width), BF16),
        pltpu.VMEM((chunks, 2, m, width), BF16),
        pltpu.VMEM((chunks, 2, m, width), BF16),
        pltpu.VMEM((chunks, m, width), BF16),
        pltpu.SemaphoreType.DMA((3, chunks)),
        pltpu.SemaphoreType.DMA((3, chunks)),
        pltpu.SemaphoreType.DMA((chunks,)),
    ]
    if teacher:
        scratch += [
            pltpu.SemaphoreType.DMA((chunks,)),
            pltpu.SemaphoreType.DMA((SECTIONS, chunks // SECTIONS)),
        ]
        shape = (
            jax.ShapeDtypeStruct((m, cols), BF16),
            jax.ShapeDtypeStruct((SECTIONS, m, cols // SECTIONS), BF16),
        )
        operands = (lhs, rhs, resid)
    else:
        shape = jax.ShapeDtypeStruct((m, cols), F32)
        operands = (lhs, rhs)
    return pl.pallas_call(
        functools.partial(scatter_kernel, teacher),
        out_shape=shape,
        in_specs=[vmem, hbm] + [vmem] * (len(operands) - 2),
        out_specs=jax.tree.map(lambda _: vmem, shape),
        scratch_shapes=scratch,
        compiler_params=pltpu.CompilerParams(
            collective_id=1 if teacher else 2, has_side_effects=True, vmem_limit_bytes=VMEM_LIMIT
        ),
        name="scatter_teacher" if teacher else "scatter_student",
    )(*operands)


def grad_kernel(
    student_proj, target, feats, proj_hbm,
    grad_s, grad_p, loss,
    proj, buf, gs, gs_out, landed, sums, sums_in, flat, back,
    g_send, g_recv, a_send, a_recv, z_send, z_recv, w_sem,
):
    section, tp, core, x, y, sib, first, second, diag = places()
    me = section * TPS + tp
    chunks, _, width = buf.shape
    rows = grad_s.shape[0]
    parts = chunks // SECTIONS
    load = pltpu.make_async_copy(proj_hbm, proj, w_sem.at[0])
    load.start()
    own = student_proj[...]
    goal = target[...].astype(F32)
    lane = lax.broadcasted_iota(jnp.int32, (own.shape[0], 128), 1)
    inner = jnp.sum(own * goal, axis=1, keepdims=True)
    own_sq = jnp.sum(own * own, axis=1, keepdims=True)
    goal_sq = jnp.sum(goal * goal, axis=1, keepdims=True)
    table = jnp.where(lane == 0, inner, jnp.where(lane == 1, own_sq, goal_sq))
    flat[...] = table.T
    sums[...] = flat[:8]
    greet_all(section, tp)

    def a_copy(d):
        other = (section + d) % SECTIONS
        return pltpu.make_async_remote_copy(
            src_ref=sums,
            dst_ref=sums_in.at[d - 1],
            send_sem=a_send.at[d - 1],
            recv_sem=a_recv.at[d - 1],
            device_id=(other, tp),
            device_id_type=MESH,
        )

    for d in (2, 1, 3):
        a_copy(d).start()
    grad_p[...] = jnp.zeros_like(grad_p)
    for d in (1, 2, 3):
        a_copy(d).wait()
    flat[:8] = sums[...] + sums_in[0] + sums_in[1] + sums_in[2]
    back[...] = flat[...].T
    table = back[...]
    inner, own_sq, goal_sq = table[:, 0:1], table[:, 1:2], table[:, 2:3]
    inv_own = lax.rsqrt(own_sq + COS_EPS)
    inv_goal = lax.rsqrt(goal_sq + COS_EPS)
    cosine = inner * inv_own * inv_goal
    loss[...] = jnp.broadcast_to(1.0 - cosine, loss.shape)
    up = LOSS_WEIGHT * (inner * inv_goal * inv_own * inv_own * inv_own)
    down = LOSS_WEIGHT * (inv_own * inv_goal)
    back[...] = jnp.where(lane == 0, up, down)

    def block_of(i):
        return (section + 2 + i // parts) % SECTIONS, i % parts

    def at_tp(index):
        return pl.ds(pl.multiple_of(index * rows, rows), rows)

    begin, forward, across, arrive, drain = gather_ops(buf, rows, g_send, g_recv)

    def make(i, carry):
        s, h = block_of(i)
        tokens = at_tp(s)
        cols = pl.ds(pl.multiple_of(h * width, width), width)
        scale = back[tokens]
        piece = (
            scale[:, 0:1] * student_proj[tokens, cols]
            - scale[:, 1:2] * target[tokens, cols].astype(F32)
        )
        buf[i, at_tp(tp)] = piece.astype(BF16)
        begin(i)
        return carry

    lax.fori_loop(0, chunks, make, 0)
    load.wait()

    def z_copy(s, step):
        other = (tp + step) % TPS
        return pltpu.make_async_remote_copy(
            src_ref=gs_out.at[s, at_tp(other)],
            dst_ref=landed.at[section, tp],
            send_sem=z_send.at[s, step],
            recv_sem=z_recv.at[section, tp],
            device_id=(s, other),
            device_id_type=MESH,
        )

    def z_land(s, t):
        place = landed.at[s, t]
        return pltpu.make_async_remote_copy(
            src_ref=place,
            dst_ref=place,
            send_sem=z_send.at[0, 0],
            recv_sem=z_recv.at[s, t],
            device_id=(section, tp),
            device_id_type=MESH,
        )

    last_dims = (((1,), (1,)), ((), ()))
    first_dims = (((0,), (0,)), ((), ()))

    def use(i):
        s, h = block_of(i)
        arrive(i)
        cols = pl.ds(pl.multiple_of(h * width, width), width)
        slopes = buf[i]
        term = lax.dot_general(slopes, proj[:, cols], last_dims, preferred_element_type=F32)

        @pl.when(h == 0)
        def _():
            gs[...] = term

        @pl.when(h > 0)
        def _():
            gs[...] += term

        @pl.when(h == parts - 1)
        def _():
            gs_out[s] = gs[...].astype(BF16)

            def push(step, carry):
                @pl.when((s != section) | (step > 0))
                def _():
                    z_copy(s, step).start()

                return carry

            lax.fori_loop(0, TPS, push, 0)

            @pl.when(s == section)
            def _():
                landed[section, tp] = gs_out[section, at_tp(tp)]

        tokens = feats[:, s].reshape(TPS * rows, feats.shape[3])
        grad_p[:, cols] += lax.dot_general(tokens, slopes, first_dims, preferred_element_type=F32)

    def step(i, carry):
        @pl.when(i < chunks)
        def _():
            forward(i)

        @pl.when((i >= 1) & (i < chunks + 1))
        def _():
            across(i - 1)

        @pl.when(i >= 2)
        def _():
            use(i - 2)

        return carry

    lax.fori_loop(0, chunks + 2, step, 0)

    def finish(i, carry):
        drain(i)
        return carry

    lax.fori_loop(0, chunks, finish, 0)

    def finish_z(i, carry):
        s, step = i // TPS, i % TPS

        @pl.when((s != section) | (step > 0))
        def _():
            z_copy(s, step).wait_send()

        @pl.when((s != section) | (step != tp))
        def _():
            z_land(s, step).wait_recv()

        return carry

    lax.fori_loop(0, SECTIONS * TPS, finish_z, 0)
    part = landed.shape[3]
    for t in range(TPS):
        total = landed[0, t].astype(F32)
        for s in range(1, SECTIONS):
            total += landed[s, t].astype(F32)
        grad_s[:, t * part : (t + 1) * part] = total


def gradients(student_proj, target, feats, proj):
    tokens, cols = student_proj.shape
    rows = tokens // SECTIONS
    part = feats.shape[3]
    chunks = 8
    width = cols * SECTIONS // chunks
    vmem = pl.BlockSpec(memory_space=pltpu.VMEM)
    hbm = pl.BlockSpec(memory_space=pl.ANY)
    dma = pltpu.SemaphoreType.DMA
    return pl.pallas_call(
        grad_kernel,
        out_shape=(
            jax.ShapeDtypeStruct((rows, part * TPS), F32),
            jax.ShapeDtypeStruct((part, cols), F32),
            jax.ShapeDtypeStruct((tokens, 128), F32),
        ),
        in_specs=[vmem, vmem, vmem, hbm],
        out_specs=(vmem, vmem, vmem),
        scratch_shapes=[
            pltpu.VMEM(proj.shape, BF16),
            pltpu.VMEM((chunks, TPS * rows, width), BF16),
            pltpu.VMEM((TPS * rows, part), F32),
            pltpu.VMEM((SECTIONS, TPS * rows, part), BF16),
            pltpu.VMEM((SECTIONS, TPS, rows, part), BF16),
            pltpu.VMEM((8, tokens), F32),
            pltpu.VMEM((SECTIONS - 1, 8, tokens), F32),
            pltpu.VMEM((128, tokens), F32),
            pltpu.VMEM((tokens, 128), F32),
            dma((7, chunks)),
            dma((7, chunks)),
            dma((SECTIONS - 1,)),
            dma((SECTIONS - 1,)),
            dma((SECTIONS, TPS)),
            dma((SECTIONS, TPS)),
            dma((1,)),
        ],
        compiler_params=pltpu.CompilerParams(
            collective_id=3, has_side_effects=True, vmem_limit_bytes=VMEM_LIMIT
        ),
        name="slope_gradients",
    )(student_proj, target, feats, proj)


def kernel_shards(
    teacher_rows,
    norm_gain,
    query_weight,
    keys_values,
    output_weight,
    doc_start,
    student_rows,
    projector,
):
    span_rows = teacher_rows[0]
    rows_float = span_rows.astype(F32)
    mean_square = jnp.mean(rows_float * rows_float, axis=1, keepdims=True)
    normed = (rows_float * lax.rsqrt(mean_square + NORM_EPS) * norm_gain[0][None, :]).astype(BF16)
    qkv, feats = project(normed, student_rows[0], query_weight[0], keys_values[0])
    q_cols = query_weight.shape[2]
    student_proj = scatter(feats.reshape(-1, feats.shape[3]), projector)
    mixed = attend(
        qkv[:, :q_cols], qkv[:, q_cols : q_cols + HD], qkv[:, q_cols + HD :], doc_start[0]
    )
    teacher_next, target = scatter(mixed, output_weight[0], span_rows)
    grad_local, grad_proj, loss_rows = gradients(
        student_proj, target.reshape(-1, target.shape[2]), feats, projector
    )
    loss_total = lax.psum(jnp.sum(loss_rows[:, 0]), "tp")
    distill_loss = loss_total / (loss_rows.shape[0] * TPS)
    return (teacher_next[None], distill_loss, grad_local[None], grad_proj)


def solution(mesh):
    fits = mesh.shape["section"] == SECTIONS and mesh.shape["tp"] == TPS
    placed = (
        P("section", "tp", None),
        P("section", None),
        P("section", None, "tp"),
        P("section", None, None, "tp"),
        P("section", "tp", None),
        P("section"),
        P("section", "tp", None),
        P("tp", "section"),
    )
    return jax.shard_map(
        kernel_shards if fits else shards,
        mesh=mesh,
        in_specs=placed,
        out_specs=(P("section", "tp", None), P(), P("section", "tp", None), P("tp", "section")),
        check_vma=False,
    )
```

```python
import functools
import math

import jax
import jax.numpy as jnp
from jax import lax
from jax.experimental import pallas as pl
from jax.experimental.pallas import tpu as pltpu
from jax.sharding import PartitionSpec as P

KVH = 8
HD = 128


LOSS_WEIGHT = 64.0
NORM_EPS = 1e-05
COS_EPS = 1e-06


def as_sent(value):
    return jax.tree.map(lambda a: a.astype(jnp.bfloat16) if a.dtype == jnp.float32 else a, value)


def partner(value, axis, apart):
    mask = 2**apart
    pairs = [(source, source ^ mask) for source in range(lax.axis_size(axis))]
    return lax.ppermute(value, axis, pairs)


def round_bf16(values):
    return lax.optimization_barrier(values.astype(jnp.bfloat16)).astype(jnp.float32)


def join_halves(mine, other, low_side):
    return jnp.where(
        low_side, jnp.concatenate([mine, other], axis=1), jnp.concatenate([other, mine], axis=1)
    )


def cosine_step(inner, own_sq, target_sq, student_proj, target):
    inv_own = lax.rsqrt(own_sq + COS_EPS)
    inv_target = lax.rsqrt(target_sq + COS_EPS)
    cosine = inner * inv_own * inv_target
    slope = LOSS_WEIGHT * (
        (inner * inv_target * inv_own * inv_own * inv_own)[:, None] * student_proj
        - target * (inv_own * inv_target)[:, None]
    )
    return (cosine, slope.astype(jnp.bfloat16))


def attend(queries, keys_full, values_full, first_new):
    row_total = queries.shape[0]
    kv_heads = keys_full.shape[1] // HD
    group = queries.shape[1] // HD // kv_heads
    query_heads = queries.reshape(row_total, kv_heads, group, HD)
    key_heads = keys_full.reshape(row_total, kv_heads, HD)
    value_heads = values_full.reshape(row_total, kv_heads, HD)
    scale = 1.0 / math.sqrt(HD)
    scores = (
        jnp.einsum("qegd,ked->egqk", query_heads, key_heads, preferred_element_type=jnp.float32)
        * scale
    )
    positions = jnp.arange(row_total, dtype=jnp.int32)
    after_start = positions >= first_new
    visible = (positions[None, :] <= positions[:, None]) & (
        after_start[None, :] == after_start[:, None]
    )
    scores = jnp.where(visible, scores, -1e30)
    row_max = jnp.max(scores, axis=-1, keepdims=True)
    expo = jnp.where(visible, jnp.exp(scores - row_max), 0.0)
    weights = (expo / jnp.sum(expo, axis=-1, keepdims=True)).astype(jnp.bfloat16)
    mixed = jnp.einsum("egqk,ked->qegd", weights, value_heads, preferred_element_type=jnp.float32)
    return mixed.astype(jnp.bfloat16).reshape(row_total, queries.shape[1])


def shards(
    teacher_rows,
    norm_gain,
    query_weight,
    keys_values,
    output_weight,
    doc_start,
    student_rows,
    projector,
):
    span_rows = teacher_rows[0]
    tp_count = lax.axis_size("tp")
    tp_position = lax.axis_index("tp")
    rows_float = span_rows.astype(jnp.float32)
    mean_square = jnp.mean(rows_float * rows_float, axis=1, keepdims=True)
    normed = (rows_float * lax.rsqrt(mean_square + NORM_EPS) * norm_gain[0][None, :]).astype(
        jnp.bfloat16
    )
    query_local = query_weight[0]
    key_local = keys_values[0, 0]
    value_local = keys_values[0, 1]
    share_count = max(1, tp_count // KVH)
    bit_total = share_count.bit_length() - 1
    query_cols = query_local.shape[1]
    key_cols = key_local.shape[1]
    block_rows = lax.all_gather(normed, "tp", axis=0, tiled=True)
    query_part = jnp.dot(block_rows, query_local, preferred_element_type=jnp.float32).astype(
        jnp.bfloat16
    )
    key_part = jnp.dot(block_rows, key_local, preferred_element_type=jnp.float32).astype(
        jnp.bfloat16
    )
    value_part = jnp.dot(block_rows, value_local, preferred_element_type=jnp.float32).astype(
        jnp.bfloat16
    )
    projected = jnp.concatenate([query_part, key_part, value_part], axis=1)
    queries = projected[:, :query_cols]
    keys_full = projected[:, query_cols : query_cols + key_cols]
    values_full = projected[:, query_cols + key_cols :]
    for bit_index in range(bit_total):
        other_key, other_value = (
            partner(as_sent(keys_full), "tp", bit_index).astype(keys_full.dtype),
            partner(as_sent(values_full), "tp", bit_index).astype(values_full.dtype),
        )
        low_side = tp_position // 2**bit_index % 2 == 0
        keys_full = join_halves(keys_full, other_key, low_side)
        values_full = join_halves(values_full, other_value, low_side)
    mixed_heads = attend(queries, keys_full, values_full, doc_start[0])
    out_local = output_weight[0]
    block = mixed_heads
    attn_sum = lax.psum_scatter(
        round_bf16(jnp.dot(block, out_local, preferred_element_type=jnp.float32)).astype(
            jnp.bfloat16
        ),
        "tp",
        scatter_dimension=0,
        tiled=True,
    ).astype(jnp.float32)
    teacher_next = (rows_float + attn_sum).astype(jnp.bfloat16)
    contract_last = (((1,), (1,)), ((), ()))
    contract_pair = (((0, 1), (0, 1)), ((), ()))
    gathered = lax.all_gather(student_rows, "section", axis=0, tiled=True)
    token_count = gathered.shape[0] * gathered.shape[1]
    token_rows = gathered.reshape(token_count, gathered.shape[2])
    arrived = lax.all_to_all(teacher_next[None], "section", split_axis=2, concat_axis=0, tiled=True)
    target = arrived.reshape(token_count, arrived.shape[2]).astype(jnp.float32)
    student_proj = jnp.dot(
        token_rows,
        lax.all_gather(projector, "tp", axis=0, tiled=True),
        preferred_element_type=jnp.float32,
    )
    inner, own_sq, target_sq = lax.psum(
        (
            jnp.sum(student_proj * target, axis=1),
            jnp.sum(student_proj * student_proj, axis=1),
            jnp.sum(target * target, axis=1),
        ),
        "section",
    )
    cosine, slope = cosine_step(inner, own_sq, target_sq, student_proj, target)
    loss_total = lax.psum(jnp.sum(1.0 - cosine), "tp")
    distill_loss = loss_total / (token_count * tp_count)
    row_terms = lax.dot_general(
        slope,
        lax.all_gather(projector, "tp", axis=0, tiled=True),
        contract_last,
        preferred_element_type=jnp.float32,
    )
    grad_local = lax.psum_scatter(
        row_terms.astype(jnp.bfloat16), "section", scatter_dimension=0, tiled=True
    ).astype(jnp.float32)
    by_column = lax.all_to_all(gathered, "tp", split_axis=2, concat_axis=1, tiled=True)
    slope_stacked = slope.reshape(gathered.shape[0], gathered.shape[1], slope.shape[1])
    block = by_column
    grad_proj = lax.dot_general(
        block,
        lax.all_gather(slope_stacked, "tp", axis=1, tiled=True),
        contract_pair,
        preferred_element_type=jnp.float32,
    )
    return (teacher_next[None], distill_loss, grad_local[None], grad_proj)


MESH = pl.DeviceIdType.MESH
F32 = jnp.float32
BF16 = jnp.bfloat16
SECTIONS = 4
TPS = 8
VMEM_LIMIT = 58 * 1024 * 1024


def places():
    section = lax.axis_index("section")
    tp = lax.axis_index("tp")
    core = tp % 2
    x = (tp // 2) % 2
    y = tp // 4
    sib = tp + 1 - 2 * core
    xn = tp + 2 - 4 * x
    yn = tp + 4 - 8 * y
    first = (1 - core) * xn + core * yn
    second = core * xn + (1 - core) * yn
    diag = xn + 4 - 8 * y
    return section, tp, core, x, y, sib, first, second, diag


def greet_lines(section, tp):
    greet(
        [(section, (tp + d) % TPS) for d in range(1, TPS)]
        + [((section + d) % SECTIONS, tp) for d in range(1, SECTIONS)]
    )


def greet(peers):
    barrier = pltpu.get_barrier_semaphore()
    for peer in peers:
        pl.semaphore_signal(barrier, inc=1, device_id=peer, device_id_type=MESH)
    pl.semaphore_wait(barrier, len(peers))


def gather_ops(buf, rows, send_sem, recv_sem):
    section, tp, core, x, y, sib, first, second, diag = places()

    def copy(kind, chunk, owner, target):
        place = buf.at[chunk, pl.ds(pl.multiple_of(owner * rows, rows), rows)]
        return pltpu.make_async_remote_copy(
            src_ref=place,
            dst_ref=place,
            send_sem=send_sem.at[kind, chunk],
            recv_sem=recv_sem.at[kind, chunk],
            device_id=(section, target),
            device_id_type=MESH,
        )

    def begin(chunk):
        copy(0, chunk, tp, first).start()
        copy(1, chunk, tp, second).start()
        copy(2, chunk, tp, sib).start()

    def forward(chunk):
        copy(0, chunk, tp, first).wait_recv()
        copy(3, chunk, first, second).start()
        copy(4, chunk, first, sib).start()
        copy(1, chunk, tp, second).wait_recv()
        copy(5, chunk, second, sib).start()

    def across(chunk):
        copy(3, chunk, first, second).wait_recv()
        copy(6, chunk, diag, sib).start()

    def arrive(chunk):
        copy(2, chunk, tp, sib).wait_recv()
        copy(4, chunk, first, sib).wait_recv()
        copy(5, chunk, second, sib).wait_recv()
        copy(6, chunk, diag, sib).wait_recv()

    def drain(chunk):
        for kind in range(7):
            copy(kind, chunk, tp, sib).wait_send()

    return begin, forward, across, arrive, drain


def project_kernel(
    span, gain, student, wq_hbm, wkv_hbm,
    qkv, feats,
    buf, wq, wkv, acc, acc_k, acc_v,
    g_send, g_recv, s_send, s_recv, z_send, z_recv, w_sem,
):
    section, tp, core, x, y, sib, first, second, diag = places()
    chunks, width = buf.shape[0], buf.shape[2]
    rows = span.shape[0]
    part = feats.shape[3]

    def wq_copy(c):
        at = pl.ds(pl.multiple_of(c * width, width), width)
        return pltpu.make_async_copy(wq_hbm.at[at], wq.at[at], w_sem.at[0, c])

    def wkv_copy(c):
        at = pl.ds(pl.multiple_of(c * width, width), width)
        return pltpu.make_async_copy(wkv_hbm.at[:, at], wkv.at[:, at], w_sem.at[1, c])

    def load(c, carry):
        wq_copy(c).start()
        wkv_copy(c).start()
        at = pl.ds(pl.multiple_of(c * width, width), width)
        values = span[:, at].astype(F32)
        return carry + jnp.sum(values * values, axis=1, keepdims=True)

    squares = lax.fori_loop(0, chunks, load, jnp.zeros((rows, 1), F32))
    inverse = lax.rsqrt(squares / (chunks * width) + NORM_EPS)

    def normalize(c, carry):
        at = pl.ds(pl.multiple_of(c * width, width), width)
        values = (span[:, at].astype(F32) * inverse * gain[:, at]).astype(BF16)
        buf[c, pl.ds(pl.multiple_of(tp * rows, rows), rows)] = values
        return carry

    lax.fori_loop(0, chunks, normalize, 0)
    feats[tp, section] = student[:, pl.ds(pl.multiple_of(tp * part, part), part)]
    acc[...] = jnp.zeros_like(acc)
    acc_k[...] = jnp.zeros_like(acc_k)
    acc_v[...] = jnp.zeros_like(acc_v)
    greet_lines(section, tp)
    begin, forward, across, arrive, drain = gather_ops(buf, rows, g_send, g_recv)

    def s_copy(step):
        other = (tp + step) % TPS
        return pltpu.make_async_remote_copy(
            src_ref=student.at[:, pl.ds(pl.multiple_of(other * part, part), part)],
            dst_ref=feats.at[tp, section],
            send_sem=s_send.at[step],
            recv_sem=s_recv.at[step],
            device_id=(section, other),
            device_id_type=MESH,
        )

    def z_copy(d):
        return pltpu.make_async_remote_copy(
            src_ref=feats.at[:, section],
            dst_ref=feats.at[:, section],
            send_sem=z_send.at[d],
            recv_sem=z_recv.at[d],
            device_id=((section + d) % SECTIONS, tp),
            device_id_type=MESH,
        )

    for d in range(1, TPS):
        s_copy(d).start()

    def start_gather(c, carry):
        begin(c)
        return carry

    lax.fori_loop(0, chunks, start_gather, 0)
    for d in range(1, TPS):
        s_copy(d).wait()
    for d in (2, 1, 3):
        z_copy(d).start()

    def step(i, carry):
        @pl.when(i < chunks)
        def _():
            forward(i)

        @pl.when((i >= 1) & (i < chunks + 1))
        def _():
            across(i - 1)

        @pl.when(i >= 2)
        def _():
            c = i - 2
            arrive(c)
            wq_copy(c).wait()
            wkv_copy(c).wait()
            at = pl.ds(pl.multiple_of(c * width, width), width)
            block = buf[c]
            acc[...] += jnp.dot(block, wq[at], preferred_element_type=F32)
            acc_k[...] += jnp.dot(block, wkv[0, at], preferred_element_type=F32)
            acc_v[...] += jnp.dot(block, wkv[1, at], preferred_element_type=F32)

        return carry

    lax.fori_loop(0, chunks + 2, step, 0)
    q_cols = acc.shape[1]
    k_cols = acc_k.shape[1]
    qkv[:, :q_cols] = acc[...].astype(BF16)
    qkv[:, q_cols : q_cols + k_cols] = acc_k[...].astype(BF16)
    qkv[:, q_cols + k_cols :] = acc_v[...].astype(BF16)

    def finish(c, carry):
        drain(c)
        return carry

    lax.fori_loop(0, chunks, finish, 0)

    for d in (1, 2, 3):
        z_copy(d).wait()


def project(span, gain, student, wq, wkv):
    rows, depth = span.shape
    total = rows * TPS
    q_cols, k_cols = wq.shape[1], wkv.shape[2]
    chunks = 8
    part = student.shape[1] // TPS
    vmem = pl.BlockSpec(memory_space=pltpu.VMEM)
    hbm = pl.BlockSpec(memory_space=pl.ANY)
    return pl.pallas_call(
        project_kernel,
        out_shape=(
            jax.ShapeDtypeStruct((total, q_cols + 2 * k_cols), BF16),
            jax.ShapeDtypeStruct((TPS, SECTIONS, rows, part), BF16),
        ),
        in_specs=[vmem, vmem, vmem, hbm, hbm],
        out_specs=(vmem, vmem),
        scratch_shapes=[
            pltpu.VMEM((chunks, total, depth // chunks), BF16),
            pltpu.VMEM(wq.shape, BF16),
            pltpu.VMEM(wkv.shape, BF16),
            pltpu.VMEM((total, q_cols), F32),
            pltpu.VMEM((total, k_cols), F32),
            pltpu.VMEM((total, k_cols), F32),
            pltpu.SemaphoreType.DMA((7, chunks)),
            pltpu.SemaphoreType.DMA((7, chunks)),
            pltpu.SemaphoreType.DMA((TPS,)),
            pltpu.SemaphoreType.DMA((TPS,)),
            pltpu.SemaphoreType.DMA((SECTIONS,)),
            pltpu.SemaphoreType.DMA((SECTIONS,)),
            pltpu.SemaphoreType.DMA((2, chunks)),
        ],
        compiler_params=pltpu.CompilerParams(
            collective_id=0, has_side_effects=True, vmem_limit_bytes=VMEM_LIMIT
        ),
        name="gather_project",
    )(span, gain, student, wq, wkv)


def scatter_kernel(
    teacher, lhs, rhs_hbm, *refs,
):
    if teacher:
        resid, out, shared = refs[:3]
        refs = refs[3:]
    else:
        out = refs[0]
        refs = refs[1:]
    rhs, part, sib_buf, pair, got1, half, got2, sends, recvs, w_sem = refs[:10]
    if teacher:
        z_send, z_recv = refs[10:]
    section, tp, core, x, y, sib, first, second, diag = places()
    chunks, _, m, width = part.shape
    f_mine = (1 - core) * x + core * y
    g_mine = core * x + (1 - core) * y

    def column(i):
        if teacher:
            return (i % SECTIONS) * (chunks // SECTIONS) + i // SECTIONS
        return i

    def columns(i):
        return pl.ds(pl.multiple_of(column(i) * width, width), width)

    def w_copy(i):
        return pltpu.make_async_copy(rhs_hbm.at[:, columns(i)], rhs.at[i], w_sem.at[i])

    def load(i, carry):
        w_copy(i).start()
        return carry

    lax.fori_loop(0, chunks, load, 0)
    peers = [(section, sib), (section, first), (section, second)]
    if teacher:
        peers += [((section + d) % SECTIONS, tp) for d in range(1, SECTIONS)]
    greet(peers)

    def remote(kind, i, source, landing, target):
        return pltpu.make_async_remote_copy(
            src_ref=source,
            dst_ref=landing,
            send_sem=sends.at[kind, i],
            recv_sem=recvs.at[kind, i],
            device_id=(section, target),
            device_id_type=MESH,
        )

    def to_sib(i):
        return remote(0, i, part.at[i, pl.ds(4 * (1 - core), 4)], sib_buf.at[i], sib)

    def to_first(i):
        return remote(1, i, pair.at[i, 1 - f_mine], got1.at[i], first)

    def to_second(i):
        return remote(2, i, half.at[i, 1 - g_mine], got2.at[i], second)

    def to_z(i, d):
        return pltpu.make_async_remote_copy(
            src_ref=out.at[:, columns(i)],
            dst_ref=shared.at[section, :, pl.ds(pl.multiple_of((i // SECTIONS) * width, width), width)],
            send_sem=z_send.at[i],
            recv_sem=z_recv.at[section, i // SECTIONS],
            device_id=(i % SECTIONS, tp),
            device_id_type=MESH,
        )

    def from_z(other, h):
        place = shared.at[other, :, pl.ds(pl.multiple_of(h * width, width), width)]
        return pltpu.make_async_remote_copy(
            src_ref=place,
            dst_ref=place,
            send_sem=z_send.at[0],
            recv_sem=z_recv.at[other, h],
            device_id=(other, tp),
            device_id_type=MESH,
        )

    def stage_a(i):
        w_copy(i).wait()
        block = jnp.dot(lhs[...], rhs[i], preferred_element_type=F32).astype(BF16)
        for t in range(TPS):
            yy, xx, cc = t // 4, (t // 2) % 2, t % 2
            slot = 4 * cc + 2 * (yy if cc else xx) + (xx if cc else yy)
            part[i, slot] = block[t * m : (t + 1) * m]
        to_sib(i).start()

    def stage_b(i):
        to_sib(i).wait_recv()
        for f in range(2):
            for g in range(2):
                mine = part[i, 4 * core + 2 * f + g].astype(F32)
                pair[i, f, g] = (mine + sib_buf[i, 2 * f + g].astype(F32)).astype(BF16)
        to_first(i).start()

    def stage_c(i):
        to_first(i).wait_recv()
        for g in range(2):
            half[i, g] = (pair[i, f_mine, g].astype(F32) + got1[i, g].astype(F32)).astype(BF16)
        to_second(i).start()

    def stage_d(i):
        to_second(i).wait_recv()
        total = half[i, g_mine].astype(F32) + got2[i].astype(F32)
        if not teacher:
            out[:, columns(i)] = total
            return
        value = (resid[:, columns(i)].astype(F32) + total).astype(BF16)
        out[:, columns(i)] = value

        @pl.when(i % SECTIONS == section)
        def _():
            at = pl.ds(pl.multiple_of((i // SECTIONS) * width, width), width)
            shared[section, :, at] = value

        @pl.when(i % SECTIONS != section)
        def _():
            to_z(i, 0).start()

    ends = (0, 1, 3, 5)

    def step(i, carry):
        for late, stage in zip(ends, (stage_a, stage_b, stage_c, stage_d)):

            @pl.when((i >= late) & (i < chunks + late))
            def _():
                stage(i - late)

        return carry

    lax.fori_loop(0, chunks + ends[-1], step, 0)

    def finish(i, carry):
        to_sib(i).wait_send()
        to_first(i).wait_send()
        to_second(i).wait_send()
        if teacher:

            @pl.when(i % SECTIONS != section)
            def _():
                to_z(i, 0).wait_send()

            @pl.when(i % SECTIONS != section)
            def _():
                from_z(i % SECTIONS, i // SECTIONS).wait_recv()

        return carry

    lax.fori_loop(0, chunks, finish, 0)


def scatter(lhs, rhs, resid=None):
    teacher = resid is not None
    depth, cols = rhs.shape
    m = lhs.shape[0] // TPS
    chunks = 8
    width = cols // chunks
    vmem = pl.BlockSpec(memory_space=pltpu.VMEM)
    hbm = pl.BlockSpec(memory_space=pl.ANY)
    scratch = [
        pltpu.VMEM((chunks, depth, width), BF16),
        pltpu.VMEM((chunks, TPS, m, width), BF16),
        pltpu.VMEM((chunks, 4, m, width), BF16),
        pltpu.VMEM((chunks, 2, 2, m, width), BF16),
        pltpu.VMEM((chunks, 2, m, width), BF16),
        pltpu.VMEM((chunks, 2, m, width), BF16),
        pltpu.VMEM((chunks, m, width), BF16),
        pltpu.SemaphoreType.DMA((3, chunks)),
        pltpu.SemaphoreType.DMA((3, chunks)),
        pltpu.SemaphoreType.DMA((chunks,)),
    ]
    if teacher:
        scratch += [
            pltpu.SemaphoreType.DMA((chunks,)),
            pltpu.SemaphoreType.DMA((SECTIONS, chunks // SECTIONS)),
        ]
        shape = (
            jax.ShapeDtypeStruct((m, cols), BF16),
            jax.ShapeDtypeStruct((SECTIONS, m, cols // SECTIONS), BF16),
        )
        operands = (lhs, rhs, resid)
    else:
        shape = jax.ShapeDtypeStruct((m, cols), F32)
        operands = (lhs, rhs)
    return pl.pallas_call(
        functools.partial(scatter_kernel, teacher),
        out_shape=shape,
        in_specs=[vmem, hbm] + [vmem] * (len(operands) - 2),
        out_specs=jax.tree.map(lambda _: vmem, shape),
        scratch_shapes=scratch,
        compiler_params=pltpu.CompilerParams(
            collective_id=1 if teacher else 2, has_side_effects=True, vmem_limit_bytes=VMEM_LIMIT
        ),
        name="scatter_teacher" if teacher else "scatter_student",
    )(*operands)


def grad_kernel(
    student_proj, target, feats, proj_hbm,
    grad_s, grad_p, loss,
    proj, buf, gs, gs_out, landed, summed, pieces, sums_in, lost, flat, back,
    g_send, g_recv, a_send, a_recv, l_send, l_recv, z_send, z_recv, p_send, p_recv, w_sem,
):
    section, tp, core, x, y, sib, first, second, diag = places()
    chunks, _, width = buf.shape
    rows = grad_s.shape[0]
    parts = chunks // SECTIONS
    load = pltpu.make_async_copy(proj_hbm, proj, w_sem.at[0])
    load.start()
    own = student_proj[...]
    goal = target[...].astype(F32)
    lane = lax.broadcasted_iota(jnp.int32, (own.shape[0], 128), 1)
    inner = jnp.sum(own * goal, axis=1, keepdims=True)
    own_sq = jnp.sum(own * own, axis=1, keepdims=True)
    goal_sq = jnp.sum(goal * goal, axis=1, keepdims=True)
    table = jnp.where(lane == 0, inner, jnp.where(lane == 1, own_sq, goal_sq))
    flat[...] = table.T
    sums_in[section] = flat[:8]
    greet_lines(section, tp)

    def a_copy(d):
        other = (section + d) % SECTIONS
        return pltpu.make_async_remote_copy(
            src_ref=sums_in.at[section],
            dst_ref=sums_in.at[section],
            send_sem=a_send.at[d - 1],
            recv_sem=a_recv.at[d - 1],
            device_id=(other, tp),
            device_id_type=MESH,
        )

    for d in (2, 1, 3):
        a_copy(d).start()
    grad_p[...] = jnp.zeros_like(grad_p)
    for d in (1, 2, 3):
        a_copy(d).wait()
    flat[:8] = sums_in[0] + sums_in[1] + sums_in[2] + sums_in[3]
    back[...] = flat[...].T
    table = back[...]
    inner, own_sq, goal_sq = table[:, 0:1], table[:, 1:2], table[:, 2:3]
    inv_own = lax.rsqrt(own_sq + COS_EPS)
    inv_goal = lax.rsqrt(goal_sq + COS_EPS)
    cosine = inner * inv_own * inv_goal
    distance = jnp.sum(jnp.broadcast_to(1.0 - cosine, back.shape), axis=0, keepdims=True)
    lost[tp] = jnp.broadcast_to(distance, loss.shape)

    def l_copy(d):
        return pltpu.make_async_remote_copy(
            src_ref=lost.at[tp],
            dst_ref=lost.at[tp],
            send_sem=l_send.at[d],
            recv_sem=l_recv.at[d],
            device_id=(section, (tp + d) % TPS),
            device_id_type=MESH,
        )

    up = LOSS_WEIGHT * (inner * inv_goal * inv_own * inv_own * inv_own)
    down = LOSS_WEIGHT * (inv_own * inv_goal)
    back[...] = jnp.where(lane == 0, up, down)

    def block_of(i):
        turn = i // parts
        late = turn // 2
        apart = (1 - late) * (2 + turn) + late * (3 - turn)
        return (section + apart) % SECTIONS, i % parts

    def at_tp(index):
        return pl.ds(pl.multiple_of(index * rows, rows), rows)

    begin, forward, across, arrive, drain = gather_ops(buf, rows, g_send, g_recv)

    def make(i, carry):
        s, h = block_of(i)
        tokens = at_tp(s)
        cols = pl.ds(pl.multiple_of(h * width, width), width)
        scale = back[tokens]
        piece = (
            scale[:, 0:1] * student_proj[tokens, cols]
            - scale[:, 1:2] * target[tokens, cols].astype(F32)
        )
        buf[i, at_tp(tp)] = piece.astype(BF16)
        begin(i)
        return carry

    lax.fori_loop(0, chunks, make, 0)
    for d in range(1, TPS):
        l_copy(d).start()
    load.wait()

    def z_copy(s):
        return pltpu.make_async_remote_copy(
            src_ref=gs_out.at[s],
            dst_ref=landed.at[section],
            send_sem=z_send.at[s],
            recv_sem=z_recv.at[section],
            device_id=(s, tp),
            device_id_type=MESH,
        )

    def z_land(s):
        return pltpu.make_async_remote_copy(
            src_ref=gs_out.at[s],
            dst_ref=landed.at[s],
            send_sem=z_send.at[s],
            recv_sem=z_recv.at[s],
            device_id=(s, tp),
            device_id_type=MESH,
        )

    def p_copy(d):
        other = (tp + d) % TPS
        return pltpu.make_async_remote_copy(
            src_ref=summed.at[at_tp(other)],
            dst_ref=pieces.at[tp],
            send_sem=p_send.at[d],
            recv_sem=p_recv.at[d],
            device_id=(section, other),
            device_id_type=MESH,
        )

    last_dims = (((1,), (1,)), ((), ()))
    first_dims = (((0,), (0,)), ((), ()))

    def use(i):
        s, h = block_of(i)
        arrive(i)
        cols = pl.ds(pl.multiple_of(h * width, width), width)
        slopes = buf[i]
        term = lax.dot_general(slopes, proj[:, cols], last_dims, preferred_element_type=F32)

        @pl.when(h == 0)
        def _():
            gs[...] = term

        @pl.when(h > 0)
        def _():
            gs[...] += term

        @pl.when(h == parts - 1)
        def _():
            gs_out[s] = gs[...].astype(BF16)

            @pl.when(s != section)
            def _():
                z_copy(s).start()

            @pl.when(s == section)
            def _():
                landed[section] = gs_out[section]

        tokens = feats[:, s].reshape(TPS * rows, feats.shape[3])
        grad_p[:, cols] += lax.dot_general(tokens, slopes, first_dims, preferred_element_type=F32)

    def step(i, carry):
        @pl.when(i < chunks)
        def _():
            forward(i)

        @pl.when((i >= 1) & (i < chunks + 1))
        def _():
            across(i - 1)

        @pl.when(i >= 2)
        def _():
            use(i - 2)

        return carry

    lax.fori_loop(0, chunks + 2, step, 0)

    for d in range(1, SECTIONS):
        z_land((section + d) % SECTIONS).wait_recv()
    total = landed[0].astype(F32)
    for s in range(1, SECTIONS):
        total += landed[s].astype(F32)
    summed[...] = total.astype(BF16)
    for d in range(1, TPS):
        p_copy(d).start()
    pieces[tp] = summed[at_tp(tp)]
    for d in range(1, TPS):
        l_copy(d).wait()
    total = lost[0]
    for t in range(1, TPS):
        total += lost[t]
    loss[...] = total / (SECTIONS * rows * TPS)

    def finish(i, carry):
        drain(i)
        return carry

    lax.fori_loop(0, chunks, finish, 0)
    for d in range(1, SECTIONS):
        z_copy((section + d) % SECTIONS).wait_send()
    for d in range(1, TPS):
        p_copy(d).wait()
    part = pieces.shape[2]
    for t in range(TPS):
        grad_s[:, t * part : (t + 1) * part] = pieces[t].astype(F32)


def gradients(student_proj, target, feats, proj):
    tokens, cols = student_proj.shape
    rows = tokens // SECTIONS
    part = feats.shape[3]
    chunks = 8
    width = cols * SECTIONS // chunks
    vmem = pl.BlockSpec(memory_space=pltpu.VMEM)
    hbm = pl.BlockSpec(memory_space=pl.ANY)
    dma = pltpu.SemaphoreType.DMA
    return pl.pallas_call(
        grad_kernel,
        out_shape=(
            jax.ShapeDtypeStruct((rows, part * TPS), F32),
            jax.ShapeDtypeStruct((part, cols), F32),
            jax.ShapeDtypeStruct((8, 128), F32),
        ),
        in_specs=[vmem, vmem, vmem, hbm],
        out_specs=(vmem, vmem, vmem),
        scratch_shapes=[
            pltpu.VMEM(proj.shape, BF16),
            pltpu.VMEM((chunks, TPS * rows, width), BF16),
            pltpu.VMEM((TPS * rows, part), F32),
            pltpu.VMEM((SECTIONS, TPS * rows, part), BF16),
            pltpu.VMEM((SECTIONS, TPS * rows, part), BF16),
            pltpu.VMEM((TPS * rows, part), BF16),
            pltpu.VMEM((TPS, rows, part), BF16),
            pltpu.VMEM((SECTIONS, 8, tokens), F32),
            pltpu.VMEM((TPS, 8, 128), F32),
            pltpu.VMEM((128, tokens), F32),
            pltpu.VMEM((tokens, 128), F32),
            dma((7, chunks)),
            dma((7, chunks)),
            dma((SECTIONS - 1,)),
            dma((SECTIONS - 1,)),
            dma((TPS,)),
            dma((TPS,)),
            dma((SECTIONS,)),
            dma((SECTIONS,)),
            dma((TPS,)),
            dma((TPS,)),
            dma((1,)),
        ],
        compiler_params=pltpu.CompilerParams(
            collective_id=3, has_side_effects=True, vmem_limit_bytes=VMEM_LIMIT
        ),
        name="slope_gradients",
    )(student_proj, target, feats, proj)


def kernel_shards(
    teacher_rows,
    norm_gain,
    query_weight,
    keys_values,
    output_weight,
    doc_start,
    student_rows,
    projector,
):
    span_rows = teacher_rows[0]
    qkv, feats = project(
        span_rows, norm_gain, student_rows[0], query_weight[0], keys_values[0]
    )
    q_cols = query_weight.shape[2]
    student_proj = scatter(feats.reshape(-1, feats.shape[3]), projector)
    mixed = attend(
        qkv[:, :q_cols], qkv[:, q_cols : q_cols + HD], qkv[:, q_cols + HD :], doc_start[0]
    )
    teacher_next, target = scatter(mixed, output_weight[0], span_rows)
    grad_local, grad_proj, loss = gradients(
        student_proj, target.reshape(-1, target.shape[2]), feats, projector
    )
    distill_loss = loss[0, 0]
    return (teacher_next[None], distill_loss, grad_local[None], grad_proj)


def solution(mesh):
    fits = mesh.shape["section"] == SECTIONS and mesh.shape["tp"] == TPS
    placed = (
        P("section", "tp", None),
        P("section", None),
        P("section", None, "tp"),
        P("section", None, None, "tp"),
        P("section", "tp", None),
        P("section"),
        P("section", "tp", None),
        P("tp", "section"),
    )
    return jax.shard_map(
        kernel_shards if fits else shards,
        mesh=mesh,
        in_specs=placed,
        out_specs=(P("section", "tp", None), P(), P("section", "tp", None), P("tp", "section")),
        check_vma=False,
    )
```

```python
import functools
import math

import jax
import jax.numpy as jnp
from jax import lax
from jax.experimental import pallas as pl
from jax.experimental.pallas import tpu as pltpu
from jax.sharding import PartitionSpec as P

KVH = 8
HD = 128


LOSS_WEIGHT = 64.0
NORM_EPS = 1e-05
COS_EPS = 1e-06


def as_sent(value):
    return jax.tree.map(lambda a: a.astype(jnp.bfloat16) if a.dtype == jnp.float32 else a, value)


def partner(value, axis, apart):
    mask = 2**apart
    pairs = [(source, source ^ mask) for source in range(lax.axis_size(axis))]
    return lax.ppermute(value, axis, pairs)


def round_bf16(values):
    return lax.optimization_barrier(values.astype(jnp.bfloat16)).astype(jnp.float32)


def join_halves(mine, other, low_side):
    return jnp.where(
        low_side, jnp.concatenate([mine, other], axis=1), jnp.concatenate([other, mine], axis=1)
    )


def cosine_step(inner, own_sq, target_sq, student_proj, target):
    inv_own = lax.rsqrt(own_sq + COS_EPS)
    inv_target = lax.rsqrt(target_sq + COS_EPS)
    cosine = inner * inv_own * inv_target
    slope = LOSS_WEIGHT * (
        (inner * inv_target * inv_own * inv_own * inv_own)[:, None] * student_proj
        - target * (inv_own * inv_target)[:, None]
    )
    return (cosine, slope.astype(jnp.bfloat16))


def attend(queries, keys_full, values_full, first_new):
    row_total = queries.shape[0]
    kv_heads = keys_full.shape[1] // HD
    group = queries.shape[1] // HD // kv_heads
    query_heads = queries.reshape(row_total, kv_heads, group, HD)
    key_heads = keys_full.reshape(row_total, kv_heads, HD)
    value_heads = values_full.reshape(row_total, kv_heads, HD)
    scale = 1.0 / math.sqrt(HD)
    scores = (
        jnp.einsum("qegd,ked->egqk", query_heads, key_heads, preferred_element_type=jnp.float32)
        * scale
    )
    positions = jnp.arange(row_total, dtype=jnp.int32)
    after_start = positions >= first_new
    visible = (positions[None, :] <= positions[:, None]) & (
        after_start[None, :] == after_start[:, None]
    )
    scores = jnp.where(visible, scores, -1e30)
    row_max = jnp.max(scores, axis=-1, keepdims=True)
    expo = jnp.where(visible, jnp.exp(scores - row_max), 0.0)
    weights = (expo / jnp.sum(expo, axis=-1, keepdims=True)).astype(jnp.bfloat16)
    mixed = jnp.einsum("egqk,ked->qegd", weights, value_heads, preferred_element_type=jnp.float32)
    return mixed.astype(jnp.bfloat16).reshape(row_total, queries.shape[1])


def shards(
    teacher_rows,
    norm_gain,
    query_weight,
    keys_values,
    output_weight,
    doc_start,
    student_rows,
    projector,
):
    span_rows = teacher_rows[0]
    tp_count = lax.axis_size("tp")
    tp_position = lax.axis_index("tp")
    rows_float = span_rows.astype(jnp.float32)
    mean_square = jnp.mean(rows_float * rows_float, axis=1, keepdims=True)
    normed = (rows_float * lax.rsqrt(mean_square + NORM_EPS) * norm_gain[0][None, :]).astype(
        jnp.bfloat16
    )
    query_local = query_weight[0]
    key_local = keys_values[0, 0]
    value_local = keys_values[0, 1]
    share_count = max(1, tp_count // KVH)
    bit_total = share_count.bit_length() - 1
    query_cols = query_local.shape[1]
    key_cols = key_local.shape[1]
    block_rows = lax.all_gather(normed, "tp", axis=0, tiled=True)
    query_part = jnp.dot(block_rows, query_local, preferred_element_type=jnp.float32).astype(
        jnp.bfloat16
    )
    key_part = jnp.dot(block_rows, key_local, preferred_element_type=jnp.float32).astype(
        jnp.bfloat16
    )
    value_part = jnp.dot(block_rows, value_local, preferred_element_type=jnp.float32).astype(
        jnp.bfloat16
    )
    projected = jnp.concatenate([query_part, key_part, value_part], axis=1)
    queries = projected[:, :query_cols]
    keys_full = projected[:, query_cols : query_cols + key_cols]
    values_full = projected[:, query_cols + key_cols :]
    for bit_index in range(bit_total):
        other_key, other_value = (
            partner(as_sent(keys_full), "tp", bit_index).astype(keys_full.dtype),
            partner(as_sent(values_full), "tp", bit_index).astype(values_full.dtype),
        )
        low_side = tp_position // 2**bit_index % 2 == 0
        keys_full = join_halves(keys_full, other_key, low_side)
        values_full = join_halves(values_full, other_value, low_side)
    mixed_heads = attend(queries, keys_full, values_full, doc_start[0])
    out_local = output_weight[0]
    block = mixed_heads
    attn_sum = lax.psum_scatter(
        round_bf16(jnp.dot(block, out_local, preferred_element_type=jnp.float32)).astype(
            jnp.bfloat16
        ),
        "tp",
        scatter_dimension=0,
        tiled=True,
    ).astype(jnp.float32)
    teacher_next = (rows_float + attn_sum).astype(jnp.bfloat16)
    contract_last = (((1,), (1,)), ((), ()))
    contract_pair = (((0, 1), (0, 1)), ((), ()))
    gathered = lax.all_gather(student_rows, "section", axis=0, tiled=True)
    token_count = gathered.shape[0] * gathered.shape[1]
    token_rows = gathered.reshape(token_count, gathered.shape[2])
    arrived = lax.all_to_all(teacher_next[None], "section", split_axis=2, concat_axis=0, tiled=True)
    target = arrived.reshape(token_count, arrived.shape[2]).astype(jnp.float32)
    student_proj = jnp.dot(
        token_rows,
        lax.all_gather(projector, "tp", axis=0, tiled=True),
        preferred_element_type=jnp.float32,
    )
    inner, own_sq, target_sq = lax.psum(
        (
            jnp.sum(student_proj * target, axis=1),
            jnp.sum(student_proj * student_proj, axis=1),
            jnp.sum(target * target, axis=1),
        ),
        "section",
    )
    cosine, slope = cosine_step(inner, own_sq, target_sq, student_proj, target)
    loss_total = lax.psum(jnp.sum(1.0 - cosine), "tp")
    distill_loss = loss_total / (token_count * tp_count)
    row_terms = lax.dot_general(
        slope,
        lax.all_gather(projector, "tp", axis=0, tiled=True),
        contract_last,
        preferred_element_type=jnp.float32,
    )
    grad_local = lax.psum_scatter(
        row_terms.astype(jnp.bfloat16), "section", scatter_dimension=0, tiled=True
    ).astype(jnp.float32)
    by_column = lax.all_to_all(gathered, "tp", split_axis=2, concat_axis=1, tiled=True)
    slope_stacked = slope.reshape(gathered.shape[0], gathered.shape[1], slope.shape[1])
    block = by_column
    grad_proj = lax.dot_general(
        block,
        lax.all_gather(slope_stacked, "tp", axis=1, tiled=True),
        contract_pair,
        preferred_element_type=jnp.float32,
    )
    return (teacher_next[None], distill_loss, grad_local[None], grad_proj)


MESH = pl.DeviceIdType.MESH
F32 = jnp.float32
BF16 = jnp.bfloat16
SECTIONS = 4
TPS = 8
VMEM_LIMIT = 58 * 1024 * 1024


def places():
    section = lax.axis_index("section")
    tp = lax.axis_index("tp")
    core = tp % 2
    x = (tp // 2) % 2
    y = tp // 4
    sib = tp + 1 - 2 * core
    xn = tp + 2 - 4 * x
    yn = tp + 4 - 8 * y
    first = (1 - core) * xn + core * yn
    second = core * xn + (1 - core) * yn
    diag = xn + 4 - 8 * y
    return section, tp, core, x, y, sib, first, second, diag


def greet_lines(section, tp):
    greet(
        [(section, (tp + d) % TPS) for d in range(1, TPS)]
        + [((section + d) % SECTIONS, tp) for d in range(1, SECTIONS)]
    )


def greet(peers):
    barrier = pltpu.get_barrier_semaphore()
    for peer in peers:
        pl.semaphore_signal(barrier, inc=1, device_id=peer, device_id_type=MESH)
    pl.semaphore_wait(barrier, len(peers))


def gather_ops(buf, rows, send_sem, recv_sem):
    section, tp, core, x, y, sib, first, second, diag = places()

    def copy(kind, chunk, owner, target):
        place = buf.at[chunk, pl.ds(pl.multiple_of(owner * rows, rows), rows)]
        return pltpu.make_async_remote_copy(
            src_ref=place,
            dst_ref=place,
            send_sem=send_sem.at[kind, chunk],
            recv_sem=recv_sem.at[kind, chunk],
            device_id=(section, target),
            device_id_type=MESH,
        )

    def begin(chunk):
        copy(0, chunk, tp, first).start()
        copy(1, chunk, tp, second).start()
        copy(2, chunk, tp, sib).start()

    def forward(chunk):
        copy(0, chunk, tp, first).wait_recv()
        copy(3, chunk, first, second).start()
        copy(4, chunk, first, sib).start()
        copy(1, chunk, tp, second).wait_recv()
        copy(5, chunk, second, sib).start()

    def across(chunk):
        copy(3, chunk, first, second).wait_recv()
        copy(6, chunk, diag, sib).start()

    def arrive(chunk):
        copy(2, chunk, tp, sib).wait_recv()
        copy(4, chunk, first, sib).wait_recv()
        copy(5, chunk, second, sib).wait_recv()
        copy(6, chunk, diag, sib).wait_recv()

    def drain(chunk):
        for kind in range(7):
            copy(kind, chunk, tp, sib).wait_send()

    return begin, forward, across, arrive, drain


def project_kernel(
    span, gain, student, wq_hbm, wkv_hbm,
    qkv, plane,
    buf, wq, wkv, acc, acc_k, acc_v,
    g_send, g_recv, s_send, s_recv, w_sem,
):
    section, tp, core, x, y, sib, first, second, diag = places()
    chunks, width = buf.shape[0], buf.shape[2]
    rows = span.shape[0]
    part = plane.shape[2]

    def wq_copy(c):
        at = pl.ds(pl.multiple_of(c * width, width), width)
        return pltpu.make_async_copy(wq_hbm.at[at], wq.at[at], w_sem.at[0, c])

    def wkv_copy(c):
        at = pl.ds(pl.multiple_of(c * width, width), width)
        return pltpu.make_async_copy(wkv_hbm.at[:, at], wkv.at[:, at], w_sem.at[1, c])

    def load(c, carry):
        wq_copy(c).start()
        wkv_copy(c).start()
        at = pl.ds(pl.multiple_of(c * width, width), width)
        values = span[:, at].astype(F32)
        return carry + jnp.sum(values * values, axis=1, keepdims=True)

    squares = lax.fori_loop(0, chunks, load, jnp.zeros((rows, 1), F32))
    inverse = lax.rsqrt(squares / (chunks * width) + NORM_EPS)

    def normalize(c, carry):
        at = pl.ds(pl.multiple_of(c * width, width), width)
        values = (span[:, at].astype(F32) * inverse * gain[:, at]).astype(BF16)
        buf[c, pl.ds(pl.multiple_of(tp * rows, rows), rows)] = values
        return carry

    lax.fori_loop(0, chunks, normalize, 0)
    plane[tp] = student[:, pl.ds(pl.multiple_of(tp * part, part), part)]
    acc[...] = jnp.zeros_like(acc)
    acc_k[...] = jnp.zeros_like(acc_k)
    acc_v[...] = jnp.zeros_like(acc_v)
    greet([(section, (tp + d) % TPS) for d in range(1, TPS)])
    begin, forward, across, arrive, drain = gather_ops(buf, rows, g_send, g_recv)

    def s_copy(step):
        other = (tp + step) % TPS
        return pltpu.make_async_remote_copy(
            src_ref=student.at[:, pl.ds(pl.multiple_of(other * part, part), part)],
            dst_ref=plane.at[tp],
            send_sem=s_send.at[step],
            recv_sem=s_recv.at[step],
            device_id=(section, other),
            device_id_type=MESH,
        )

    for d in range(1, TPS):
        s_copy(d).start()

    def start_gather(c, carry):
        begin(c)
        return carry

    lax.fori_loop(0, chunks, start_gather, 0)

    def step(i, carry):
        @pl.when(i < chunks)
        def _():
            forward(i)

        @pl.when((i >= 1) & (i < chunks + 1))
        def _():
            across(i - 1)

        @pl.when(i >= 2)
        def _():
            c = i - 2
            arrive(c)
            wq_copy(c).wait()
            wkv_copy(c).wait()
            at = pl.ds(pl.multiple_of(c * width, width), width)
            block = buf[c]
            acc[...] += jnp.dot(block, wq[at], preferred_element_type=F32)
            acc_k[...] += jnp.dot(block, wkv[0, at], preferred_element_type=F32)
            acc_v[...] += jnp.dot(block, wkv[1, at], preferred_element_type=F32)

        return carry

    lax.fori_loop(0, chunks + 2, step, 0)
    q_cols = acc.shape[1]
    k_cols = acc_k.shape[1]
    qkv[:, :q_cols] = acc[...].astype(BF16)
    qkv[:, q_cols : q_cols + k_cols] = acc_k[...].astype(BF16)
    qkv[:, q_cols + k_cols :] = acc_v[...].astype(BF16)

    def finish(c, carry):
        drain(c)
        return carry

    lax.fori_loop(0, chunks, finish, 0)

    for d in range(1, TPS):
        s_copy(d).wait()


def project(span, gain, student, wq, wkv):
    rows, depth = span.shape
    total = rows * TPS
    q_cols, k_cols = wq.shape[1], wkv.shape[2]
    chunks = 8
    part = student.shape[1] // TPS
    vmem = pl.BlockSpec(memory_space=pltpu.VMEM)
    hbm = pl.BlockSpec(memory_space=pl.ANY)
    return pl.pallas_call(
        project_kernel,
        out_shape=(
            jax.ShapeDtypeStruct((total, q_cols + 2 * k_cols), BF16),
            jax.ShapeDtypeStruct((TPS, rows, part), BF16),
        ),
        in_specs=[vmem, vmem, vmem, hbm, hbm],
        out_specs=(vmem, vmem),
        scratch_shapes=[
            pltpu.VMEM((chunks, total, depth // chunks), BF16),
            pltpu.VMEM(wq.shape, BF16),
            pltpu.VMEM(wkv.shape, BF16),
            pltpu.VMEM((total, q_cols), F32),
            pltpu.VMEM((total, k_cols), F32),
            pltpu.VMEM((total, k_cols), F32),
            pltpu.SemaphoreType.DMA((7, chunks)),
            pltpu.SemaphoreType.DMA((7, chunks)),
            pltpu.SemaphoreType.DMA((TPS,)),
            pltpu.SemaphoreType.DMA((TPS,)),
            pltpu.SemaphoreType.DMA((2, chunks)),
        ],
        compiler_params=pltpu.CompilerParams(
            collective_id=0, has_side_effects=True, vmem_limit_bytes=VMEM_LIMIT
        ),
        name="gather_project",
    )(span, gain, student, wq, wkv)


def scatter_kernel(
    teacher, lhs, rhs_hbm, *refs,
):
    if teacher:
        resid, moved, out, shared = refs[:4]
        refs = refs[4:]
    else:
        moved, out, shared = refs[:3]
        refs = refs[3:]
    rhs, part, sib_buf, pair, got1, half, got2, sends, recvs, w_sem, z_send, z_recv = refs
    section, tp, core, x, y, sib, first, second, diag = places()
    chunks, _, m, width = part.shape
    f_mine = (1 - core) * x + core * y
    g_mine = core * x + (1 - core) * y

    def columns(i):
        return pl.ds(pl.multiple_of(i * width, width), width)

    def w_copy(i):
        return pltpu.make_async_copy(rhs_hbm.at[:, columns(i)], rhs.at[i], w_sem.at[i])

    def load(i, carry):
        w_copy(i).start()
        return carry

    lax.fori_loop(0, chunks, load, 0)
    peers = [(section, sib), (section, first), (section, second)]
    peers += [((section + d) % SECTIONS, tp) for d in range(1, SECTIONS)]
    if teacher:
        shared[:, section] = moved[...]
    else:
        span = shared.shape[2]
        shared[section] = moved[:, pl.ds(pl.multiple_of(section * span, span), span)]
    greet(peers)

    def z_copy(d):
        other = (section + d) % SECTIONS
        if teacher:
            source, landing = moved, shared.at[:, section]
        else:
            source = moved.at[:, pl.ds(pl.multiple_of(other * span, span), span)]
            landing = shared.at[section]
        return pltpu.make_async_remote_copy(
            src_ref=source,
            dst_ref=landing,
            send_sem=z_send.at[d],
            recv_sem=z_recv.at[d],
            device_id=(other, tp),
            device_id_type=MESH,
        )

    for d in (2, 1, 3):
        z_copy(d).start()

    def remote(kind, i, source, landing, target):
        return pltpu.make_async_remote_copy(
            src_ref=source,
            dst_ref=landing,
            send_sem=sends.at[kind, i],
            recv_sem=recvs.at[kind, i],
            device_id=(section, target),
            device_id_type=MESH,
        )

    def to_sib(i):
        return remote(0, i, part.at[i, pl.ds(4 * (1 - core), 4)], sib_buf.at[i], sib)

    def to_first(i):
        return remote(1, i, pair.at[i, 1 - f_mine], got1.at[i], first)

    def to_second(i):
        return remote(2, i, half.at[i, 1 - g_mine], got2.at[i], second)

    def stage_a(i):
        w_copy(i).wait()
        block = jnp.dot(lhs[...], rhs[i], preferred_element_type=F32).astype(BF16)
        for t in range(TPS):
            yy, xx, cc = t // 4, (t // 2) % 2, t % 2
            slot = 4 * cc + 2 * (yy if cc else xx) + (xx if cc else yy)
            part[i, slot] = block[t * m : (t + 1) * m]
        to_sib(i).start()

    def stage_b(i):
        to_sib(i).wait_recv()
        for f in range(2):
            for g in range(2):
                mine = part[i, 4 * core + 2 * f + g].astype(F32)
                pair[i, f, g] = (mine + sib_buf[i, 2 * f + g].astype(F32)).astype(BF16)
        to_first(i).start()

    def stage_c(i):
        to_first(i).wait_recv()
        for g in range(2):
            half[i, g] = (pair[i, f_mine, g].astype(F32) + got1[i, g].astype(F32)).astype(BF16)
        to_second(i).start()

    def stage_d(i):
        to_second(i).wait_recv()
        total = half[i, g_mine].astype(F32) + got2[i].astype(F32)
        if not teacher:
            out[:, columns(i)] = total
            return
        out[:, columns(i)] = (resid[:, columns(i)].astype(F32) + total).astype(BF16)

    ends = (0, 1, 3, 5)

    def step(i, carry):
        for late, stage in zip(ends, (stage_a, stage_b, stage_c, stage_d)):

            @pl.when((i >= late) & (i < chunks + late))
            def _():
                stage(i - late)

        return carry

    lax.fori_loop(0, chunks + ends[-1], step, 0)

    def finish(i, carry):
        to_sib(i).wait_send()
        to_first(i).wait_send()
        to_second(i).wait_send()
        return carry

    lax.fori_loop(0, chunks, finish, 0)
    for d in (1, 2, 3):
        z_copy(d).wait()


def scatter(lhs, rhs, moved, resid=None):
    teacher = resid is not None
    depth, cols = rhs.shape
    m = lhs.shape[0] // TPS
    chunks = 8
    width = cols // chunks
    vmem = pl.BlockSpec(memory_space=pltpu.VMEM)
    hbm = pl.BlockSpec(memory_space=pl.ANY)
    scratch = [
        pltpu.VMEM((chunks, depth, width), BF16),
        pltpu.VMEM((chunks, TPS, m, width), BF16),
        pltpu.VMEM((chunks, 4, m, width), BF16),
        pltpu.VMEM((chunks, 2, 2, m, width), BF16),
        pltpu.VMEM((chunks, 2, m, width), BF16),
        pltpu.VMEM((chunks, 2, m, width), BF16),
        pltpu.VMEM((chunks, m, width), BF16),
        pltpu.SemaphoreType.DMA((3, chunks)),
        pltpu.SemaphoreType.DMA((3, chunks)),
        pltpu.SemaphoreType.DMA((chunks,)),
        pltpu.SemaphoreType.DMA((SECTIONS,)),
        pltpu.SemaphoreType.DMA((SECTIONS,)),
    ]
    if teacher:
        shape = (
            jax.ShapeDtypeStruct((m, cols), BF16),
            jax.ShapeDtypeStruct((TPS, SECTIONS) + moved.shape[1:], BF16),
        )
        operands = (lhs, rhs, resid, moved)
    else:
        shape = (
            jax.ShapeDtypeStruct((m, cols), F32),
            jax.ShapeDtypeStruct((SECTIONS, moved.shape[0], cols), BF16),
        )
        operands = (lhs, rhs, moved)
    return pl.pallas_call(
        functools.partial(scatter_kernel, teacher),
        out_shape=shape,
        in_specs=[vmem, hbm] + [vmem] * (len(operands) - 2),
        out_specs=jax.tree.map(lambda _: vmem, shape),
        scratch_shapes=scratch,
        compiler_params=pltpu.CompilerParams(
            collective_id=1 if teacher else 2, has_side_effects=True, vmem_limit_bytes=VMEM_LIMIT
        ),
        name="scatter_teacher" if teacher else "scatter_student",
    )(*operands)


def grad_kernel(
    student_proj, target, feats, proj_hbm,
    grad_s, grad_p, loss,
    proj, buf, gs, gs_out, landed, summed, pieces, sums_in, lost, flat, back,
    g_send, g_recv, a_send, a_recv, l_send, l_recv, z_send, z_recv, p_send, p_recv, w_sem,
):
    section, tp, core, x, y, sib, first, second, diag = places()
    chunks, _, width = buf.shape
    rows = grad_s.shape[0]
    parts = chunks // SECTIONS
    load = pltpu.make_async_copy(proj_hbm, proj, w_sem.at[0])
    load.start()
    own = student_proj[...]
    goal = target[...].astype(F32)
    lane = lax.broadcasted_iota(jnp.int32, (own.shape[0], 128), 1)
    inner = jnp.sum(own * goal, axis=1, keepdims=True)
    own_sq = jnp.sum(own * own, axis=1, keepdims=True)
    goal_sq = jnp.sum(goal * goal, axis=1, keepdims=True)
    table = jnp.where(lane == 0, inner, jnp.where(lane == 1, own_sq, goal_sq))
    flat[...] = table.T
    sums_in[section] = flat[:8]
    greet_lines(section, tp)

    def a_copy(d):
        other = (section + d) % SECTIONS
        return pltpu.make_async_remote_copy(
            src_ref=sums_in.at[section],
            dst_ref=sums_in.at[section],
            send_sem=a_send.at[d - 1],
            recv_sem=a_recv.at[d - 1],
            device_id=(other, tp),
            device_id_type=MESH,
        )

    for d in (2, 1, 3):
        a_copy(d).start()
    grad_p[...] = jnp.zeros_like(grad_p)
    for d in (1, 2, 3):
        a_copy(d).wait()
    flat[:8] = sums_in[0] + sums_in[1] + sums_in[2] + sums_in[3]
    back[...] = flat[...].T
    table = back[...]
    inner, own_sq, goal_sq = table[:, 0:1], table[:, 1:2], table[:, 2:3]
    inv_own = lax.rsqrt(own_sq + COS_EPS)
    inv_goal = lax.rsqrt(goal_sq + COS_EPS)
    cosine = inner * inv_own * inv_goal
    distance = jnp.sum(jnp.broadcast_to(1.0 - cosine, back.shape), axis=0, keepdims=True)
    lost[tp] = jnp.broadcast_to(distance, loss.shape)

    def l_copy(d):
        return pltpu.make_async_remote_copy(
            src_ref=lost.at[tp],
            dst_ref=lost.at[tp],
            send_sem=l_send.at[d],
            recv_sem=l_recv.at[d],
            device_id=(section, (tp + d) % TPS),
            device_id_type=MESH,
        )

    up = LOSS_WEIGHT * (inner * inv_goal * inv_own * inv_own * inv_own)
    down = LOSS_WEIGHT * (inv_own * inv_goal)
    back[...] = jnp.where(lane == 0, up, down)

    def block_of(i):
        turn = i // parts
        late = turn // 2
        apart = (1 - late) * (2 + turn) + late * (3 - turn)
        return (section + apart) % SECTIONS, i % parts

    def at_tp(index):
        return pl.ds(pl.multiple_of(index * rows, rows), rows)

    begin, forward, across, arrive, drain = gather_ops(buf, rows, g_send, g_recv)

    def make(i, carry):
        s, h = block_of(i)
        tokens = at_tp(s)
        cols = pl.ds(pl.multiple_of(h * width, width), width)
        scale = back[tokens]
        piece = (
            scale[:, 0:1] * student_proj[tokens, cols]
            - scale[:, 1:2] * target[tokens, cols].astype(F32)
        )
        buf[i, at_tp(tp)] = piece.astype(BF16)
        begin(i)
        return carry

    lax.fori_loop(0, chunks, make, 0)
    for d in range(1, TPS):
        l_copy(d).start()
    load.wait()

    def z_copy(s):
        return pltpu.make_async_remote_copy(
            src_ref=gs_out.at[s],
            dst_ref=landed.at[section],
            send_sem=z_send.at[s],
            recv_sem=z_recv.at[section],
            device_id=(s, tp),
            device_id_type=MESH,
        )

    def z_land(s):
        return pltpu.make_async_remote_copy(
            src_ref=gs_out.at[s],
            dst_ref=landed.at[s],
            send_sem=z_send.at[s],
            recv_sem=z_recv.at[s],
            device_id=(s, tp),
            device_id_type=MESH,
        )

    def p_copy(d):
        other = (tp + d) % TPS
        return pltpu.make_async_remote_copy(
            src_ref=summed.at[at_tp(other)],
            dst_ref=pieces.at[tp],
            send_sem=p_send.at[d],
            recv_sem=p_recv.at[d],
            device_id=(section, other),
            device_id_type=MESH,
        )

    last_dims = (((1,), (1,)), ((), ()))
    first_dims = (((0,), (0,)), ((), ()))

    def use(i):
        s, h = block_of(i)
        arrive(i)
        cols = pl.ds(pl.multiple_of(h * width, width), width)
        slopes = buf[i]
        term = lax.dot_general(slopes, proj[:, cols], last_dims, preferred_element_type=F32)

        @pl.when(h == 0)
        def _():
            gs[...] = term

        @pl.when(h > 0)
        def _():
            gs[...] += term

        @pl.when(h == parts - 1)
        def _():
            gs_out[s] = gs[...].astype(BF16)

            @pl.when(s != section)
            def _():
                z_copy(s).start()

            @pl.when(s == section)
            def _():
                landed[section] = gs_out[section]

        tokens = feats[:, s].reshape(TPS * rows, feats.shape[3])
        grad_p[:, cols] += lax.dot_general(tokens, slopes, first_dims, preferred_element_type=F32)

    def step(i, carry):
        @pl.when(i < chunks)
        def _():
            forward(i)

        @pl.when((i >= 1) & (i < chunks + 1))
        def _():
            across(i - 1)

        @pl.when(i >= 2)
        def _():
            use(i - 2)

        return carry

    lax.fori_loop(0, chunks + 2, step, 0)

    for d in range(1, SECTIONS):
        z_land((section + d) % SECTIONS).wait_recv()
    total = landed[0].astype(F32)
    for s in range(1, SECTIONS):
        total += landed[s].astype(F32)
    summed[...] = total.astype(BF16)
    for d in range(1, TPS):
        p_copy(d).start()
    pieces[tp] = summed[at_tp(tp)]
    for d in range(1, TPS):
        l_copy(d).wait()
    total = lost[0]
    for t in range(1, TPS):
        total += lost[t]
    loss[...] = total / (SECTIONS * rows * TPS)

    def finish(i, carry):
        drain(i)
        return carry

    lax.fori_loop(0, chunks, finish, 0)
    for d in range(1, SECTIONS):
        z_copy((section + d) % SECTIONS).wait_send()
    for d in range(1, TPS):
        p_copy(d).wait()
    part = pieces.shape[2]
    for t in range(TPS):
        grad_s[:, t * part : (t + 1) * part] = pieces[t].astype(F32)


def gradients(student_proj, target, feats, proj):
    tokens, cols = student_proj.shape
    rows = tokens // SECTIONS
    part = feats.shape[3]
    chunks = 8
    width = cols * SECTIONS // chunks
    vmem = pl.BlockSpec(memory_space=pltpu.VMEM)
    hbm = pl.BlockSpec(memory_space=pl.ANY)
    dma = pltpu.SemaphoreType.DMA
    return pl.pallas_call(
        grad_kernel,
        out_shape=(
            jax.ShapeDtypeStruct((rows, part * TPS), F32),
            jax.ShapeDtypeStruct((part, cols), F32),
            jax.ShapeDtypeStruct((8, 128), F32),
        ),
        in_specs=[vmem, vmem, vmem, hbm],
        out_specs=(vmem, vmem, vmem),
        scratch_shapes=[
            pltpu.VMEM(proj.shape, BF16),
            pltpu.VMEM((chunks, TPS * rows, width), BF16),
            pltpu.VMEM((TPS * rows, part), F32),
            pltpu.VMEM((SECTIONS, TPS * rows, part), BF16),
            pltpu.VMEM((SECTIONS, TPS * rows, part), BF16),
            pltpu.VMEM((TPS * rows, part), BF16),
            pltpu.VMEM((TPS, rows, part), BF16),
            pltpu.VMEM((SECTIONS, 8, tokens), F32),
            pltpu.VMEM((TPS, 8, 128), F32),
            pltpu.VMEM((128, tokens), F32),
            pltpu.VMEM((tokens, 128), F32),
            dma((7, chunks)),
            dma((7, chunks)),
            dma((SECTIONS - 1,)),
            dma((SECTIONS - 1,)),
            dma((TPS,)),
            dma((TPS,)),
            dma((SECTIONS,)),
            dma((SECTIONS,)),
            dma((TPS,)),
            dma((TPS,)),
            dma((1,)),
        ],
        compiler_params=pltpu.CompilerParams(
            collective_id=3, has_side_effects=True, vmem_limit_bytes=VMEM_LIMIT
        ),
        name="slope_gradients",
    )(student_proj, target, feats, proj)


def kernel_shards(
    teacher_rows,
    norm_gain,
    query_weight,
    keys_values,
    output_weight,
    doc_start,
    student_rows,
    projector,
):
    span_rows = teacher_rows[0]
    qkv, plane = project(
        span_rows, norm_gain, student_rows[0], query_weight[0], keys_values[0]
    )
    q_cols = query_weight.shape[2]
    mixed = attend(
        qkv[:, :q_cols], qkv[:, q_cols : q_cols + HD], qkv[:, q_cols + HD :], doc_start[0]
    )
    teacher_next, feats = scatter(mixed, output_weight[0], plane, span_rows)
    student_proj, target = scatter(feats.reshape(-1, feats.shape[3]), projector, teacher_next)
    grad_local, grad_proj, loss = gradients(
        student_proj, target.reshape(-1, target.shape[2]), feats, projector
    )
    distill_loss = loss[0, 0]
    return (teacher_next[None], distill_loss, grad_local[None], grad_proj)


def solution(mesh):
    fits = mesh.shape["section"] == SECTIONS and mesh.shape["tp"] == TPS
    placed = (
        P("section", "tp", None),
        P("section", None),
        P("section", None, "tp"),
        P("section", None, None, "tp"),
        P("section", "tp", None),
        P("section"),
        P("section", "tp", None),
        P("tp", "section"),
    )
    return jax.shard_map(
        kernel_shards if fits else shards,
        mesh=mesh,
        in_specs=placed,
        out_specs=(P("section", "tp", None), P(), P("section", "tp", None), P("tp", "section")),
        check_vma=False,
    )
```
